256 devices in a mesh: grp: 8 (over y, core), seq: 32 (over z, x).
Axes of the slice: x: 4, y: 4, z: 8, core: 2. Of those that a mesh axis runs over, the one named last changes fastest.
Arguments:
- query_rows: bfloat16 [1, 32768, 1024], P(None, ('grp', 'seq')), may hold values from -6 to 6
- key_rows: bfloat16 [1, 32768, 1024], P(None, ('grp', 'seq')), may hold values from -6 to 6
- value_rows: bfloat16 [1, 32768, 1024], P(None, ('grp', 'seq')), may hold values from -6 to 6
- teacher: bfloat16 [1, 32768, 1024], P(None, ('grp', 'seq')), may hold values from -4 to 4
- query_map: bfloat16 [8, 128, 64], replicated, may hold values from -0.5 to 0.5
- key_map: bfloat16 [8, 128, 64], replicated, may hold values from -0.5 to 0.5
- decay_rate: float32 [1, 8, 32768], P(None, None, ('grp', 'seq')), may hold values from 0 to 1, as said below
Outputs:
- mismatch: float32 [1, 32768, 1024], P(None, ('grp', 'seq'))
The draws below stay inside these ranges and needn't reach their ends.
Inputs may be any that keep to these rules, and one draw needn't show every extreme that they name: `decay_rate`: rates are non-negative; a state is multiplied by exp(-rate) at each position.
All inputs are finite; a program needn't handle non-finite values.
Results may differ from the reference program's by a relative error of at most 0.00037.
Values sent between devices are 32-bit elements; how exact they have to be, the bound alone decides.
A program may use at most 256 MiB of HBM per device.

```python
import math
import jax
import jax.numpy as jnp
from jax import lax

H = 8
DH = 128
FH = 64
SEQUENCE_COUNT = 1
TOK_DEV = 128
TOKEN_COUNT = 32768


def draw_decay_rate(key, part):
    key = jax.random.fold_in(key, 7)
    random_subkeys = jax.random.split(key, 10)
    regime_count = max(1, H // 4)
    fast_count = H // 4
    block_count = TOKEN_COUNT // TOK_DEV
    head_rank = jax.random.permutation(random_subkeys[0], H)[None, :, None]
    regime_heads = head_rank < regime_count
    fast_heads = jnp.logical_and(head_rank >= regime_count, head_rank < regime_count + fast_count)
    fast_rate = jnp.exp(jax.random.uniform(random_subkeys[1], (SEQUENCE_COUNT, H, 1), minval=math.log(1.0 / 50.0), maxval=math.log(1.0 / 30.0)))
    base_rate = jnp.where(fast_heads, fast_rate, 0.5 / TOKEN_COUNT)
    per_block = jnp.exp(jax.random.uniform(random_subkeys[2], (SEQUENCE_COUNT, H, block_count, 1), minval=math.log(0.5), maxval=math.log(2.0)))
    per_block = jnp.broadcast_to(per_block, (SEQUENCE_COUNT, H, block_count, TOK_DEV)).reshape(SEQUENCE_COUNT, H, TOKEN_COUNT)
    per_position = jnp.exp(jax.random.uniform(random_subkeys[3], (SEQUENCE_COUNT, H, TOKEN_COUNT), minval=math.log(0.5), maxval=math.log(2.0)))
    positions = jnp.arange(TOKEN_COUNT)[None, None, :]
    stretch_blocks = max(4, 128 // TOK_DEV)
    stretch_low = min(block_count // 2, block_count - stretch_blocks - 1)
    stretch_start = jax.random.randint(random_subkeys[4], (SEQUENCE_COUNT, 1, 1), stretch_low, block_count - stretch_blocks) * TOK_DEV
    inside = jnp.logical_and(positions >= stretch_start, positions < stretch_start + stretch_blocks * TOK_DEV)
    stretch_total = jax.random.uniform(random_subkeys[5], (SEQUENCE_COUNT, H, 1), minval=8.0, maxval=10.0)
    stretch_rate = jnp.where(jnp.logical_and(regime_heads, inside), stretch_total / (stretch_blocks * TOK_DEV), 0.0)
    spike_block = jax.random.randint(random_subkeys[6], (SEQUENCE_COUNT, 1, 1, 1), block_count // 4, block_count)
    offset_first = jax.random.randint(random_subkeys[7], (SEQUENCE_COUNT, 1, 1, 1), 0, TOK_DEV // 2)
    offset_second = jax.random.randint(random_subkeys[8], (SEQUENCE_COUNT, 1, 1, 1), TOK_DEV // 2, TOK_DEV)
    spike_locations = jnp.concatenate([spike_block * TOK_DEV + offset_first, spike_block * TOK_DEV + offset_second], axis=2)
    dropout_fraction = jax.random.uniform(random_subkeys[9], (SEQUENCE_COUNT, H, 2, 1), minval=0.47, maxval=0.5)
    spike_positions = jnp.arange(TOKEN_COUNT)[None, None, None, :] == spike_locations
    abrupt_decay_drop = jnp.sum(jnp.where(spike_positions, -jnp.log(1.0 - dropout_fraction), 0.0), axis=2)
    total_rate = (base_rate * per_block + stretch_rate) * per_position + abrupt_decay_drop
    return jnp.minimum(total_rate, 1.0).astype(jnp.float32)


def shard_levels(own_key, extent, cuts, least, high):
    factor_of = 1.0
    for dim, shards_of in cuts:
        steps = jax.random.uniform(jax.random.fold_in(jax.random.fold_in(own_key, 6), dim), (shards_of,), jnp.float32, least / len(cuts), high / len(cuts))
        factor_of = factor_of * jnp.repeat(jnp.exp(steps), extent[dim] // shards_of).reshape((-1,) + (1,) * (len(extent) - 1 - dim))
    return factor_of


def normal_values(own_key, extent, width, limit, cuts=(), held_as=jnp.bfloat16):
    drawn = width * jax.random.normal(own_key, extent, jnp.float32)
    if cuts:
        drawn = drawn * shard_levels(own_key, extent, cuts, -0.22, 0.18)
    return jnp.clip(drawn, -limit, limit).astype(held_as)


def setup_inputs(seed: int = 0) -> dict:
    splits = jax.random.split(jax.random.key(seed), 8)
    query_rows = normal_values(splits[0], (SEQUENCE_COUNT, TOKEN_COUNT, H * DH), 1.0, 6.0, ((1, 256),))
    key_rows = normal_values(splits[1], (SEQUENCE_COUNT, TOKEN_COUNT, H * DH), 1.0, 6.0, ((1, 256),))
    value_rows = normal_values(splits[2], (SEQUENCE_COUNT, TOKEN_COUNT, H * DH), 1.0, 6.0, ((1, 256),))
    teacher = normal_values(splits[3], (SEQUENCE_COUNT, TOKEN_COUNT, H * DH), 0.5, 4.0, ((1, 256),))
    query_map = normal_values(splits[4], (H, DH, FH), DH ** -0.5, 0.5)
    key_map = normal_values(splits[5], (H, DH, FH), DH ** -0.5, 0.5)
    decay_rate = draw_decay_rate(jax.random.fold_in(splits[7], 71), 0)
    return {"query_rows": query_rows, "key_rows": key_rows, "value_rows": value_rows, "teacher": teacher, "query_map": query_map, "key_map": key_map, "decay_rate": decay_rate}


def feature_map(rows, weight):
    sequences, length, row_width = rows.shape
    head_count, head_size, feature_half = weight.shape
    split_rows = rows.reshape(sequences, length, head_count, head_size).astype(jnp.float32)
    projected = jnp.einsum("sthd,hdf->sthf", split_rows, weight.astype(jnp.float32))
    both = jnp.concatenate([jax.nn.softplus(projected), jax.nn.softplus(-projected)], axis=-1)
    return both.astype(jnp.bfloat16)


def block_terms(query_phi, key_phi, value_rows, rate_block):
    sequences, length, head_count, feature_count = key_phi.shape
    split_values = value_rows.reshape(sequences, length, head_count, -1)
    running = jnp.cumsum(rate_block, axis=-1)
    block_sum = running[..., -1:]
    scores = jnp.einsum("sthf,suhf->shtu", query_phi.astype(jnp.float32), key_phi.astype(jnp.float32))
    spacing = running[..., :, None] - running[..., None, :]
    causal = jnp.arange(length)[:, None] >= jnp.arange(length)[None, :]
    weighted = jnp.where(causal, scores * jnp.exp(-jnp.where(causal, spacing, 0.0)), 0.0)
    denominator = jnp.sum(weighted, axis=-1)
    weighted_round = lax.optimization_barrier(weighted.astype(jnp.bfloat16)).astype(jnp.float32)
    numerator = jnp.einsum("shtu,suhd->sthd", weighted_round, split_values.astype(jnp.float32))
    fade = jnp.exp(-(block_sum - running))
    faded = key_phi.astype(jnp.float32) * jnp.transpose(fade, (0, 2, 1))[..., None]
    norm_part = jnp.sum(faded, axis=1)
    faded_round = lax.optimization_barrier(faded.astype(jnp.bfloat16)).astype(jnp.float32)
    state_part = jnp.einsum("sthf,sthd->shfd", faded_round, split_values.astype(jnp.float32))
    decay_out = jnp.exp(-block_sum[..., 0])
    return numerator, denominator, (decay_out, state_part, norm_part), running


def combine(earlier, later):
    decay_first, state_first, norm_first = earlier
    decay_second, state_second, norm_second = later
    return (decay_first * decay_second,
            decay_second[..., None, None] * state_first + state_second,
            decay_second[..., None] * norm_first + norm_second)


def finish(query_phi, running, numerator, denominator, carried, teacher):
    decay_in, state_in, norm_in = carried
    lead_decay = jnp.transpose(jnp.exp(-running), (0, 2, 1))
    phi_wide = query_phi.astype(jnp.float32)
    from_state = jnp.einsum("sthf,shfd->sthd", phi_wide, state_in, precision=lax.Precision.HIGHEST)
    from_norm = jnp.einsum("sthf,shf->sth", phi_wide, norm_in, precision=lax.Precision.HIGHEST)
    total_num = numerator + lead_decay[..., None] * from_state
    total_den = jnp.transpose(denominator, (0, 2, 1)) + lead_decay * from_norm
    student = total_num / total_den[..., None]
    return student.reshape(teacher.shape) - teacher.astype(jnp.float32)


def reference(query_rows, key_rows, value_rows, teacher, query_map, key_map, decay_rate):
    sequences, length_all, row_width = query_rows.shape
    head_count, head_size, feature_half = query_map.shape
    blocks = length_all // TOK_DEV

    def to_blocks(array):
        return array.reshape(sequences, blocks, TOK_DEV, row_width).transpose(1, 0, 2, 3)

    rate_blocks = decay_rate.reshape(sequences, head_count, blocks, TOK_DEV).transpose(2, 0, 1, 3)

    def advance(carried, pieces):
        query_block, key_block, value_block, teacher_block, rate_block = pieces
        query_phi = feature_map(query_block, query_map)
        key_phi = feature_map(key_block, key_map)
        numerator, denominator, own_summary, running = block_terms(query_phi, key_phi, value_block, rate_block)
        block_out = finish(query_phi, running, numerator, denominator, carried, teacher_block)
        return combine(carried, own_summary), block_out

    start_state = (jnp.ones((sequences, head_count), jnp.float32),
                   jnp.zeros((sequences, head_count, 2 * feature_half, head_size), jnp.float32),
                   jnp.zeros((sequences, head_count, 2 * feature_half), jnp.float32))
    pieces = (to_blocks(query_rows), to_blocks(key_rows), to_blocks(value_rows), to_blocks(teacher), rate_blocks)
    final_state, all_blocks = lax.scan(advance, start_state, pieces)
    return all_blocks.transpose(1, 0, 2, 3).reshape(sequences, length_all, row_width)
```

```python
import functools

import jax
import jax.numpy as jnp
from jax import lax
from jax.experimental import pallas as pl
from jax.experimental.pallas import tpu as pltpu
from jax.sharding import PartitionSpec as P

MESH = pl.DeviceIdType.MESH
F32 = jnp.float32
BF16 = jnp.bfloat16

NX, NZ, NG = 4, 8, 8
HEADS = 8
T = 128
SLICE = HEADS * T // (NX * NZ)
PER_HEAD = T // SLICE


def softplus(p):
    return jnp.maximum(p, 0.0) + jnp.log1p(jnp.exp(-jnp.abs(p)))


def dot(a, b, dims=((1,), (0,))):
    return lax.dot_general(a, b, (dims, ((), ())), preferred_element_type=F32)


def kernel(
    q_ref, k_ref, v_ref, t_ref, wq_ref, wk_ref, rate_ref, o_ref,
    own, xin, tout, zin, gin, wout, cin, vout, fin,
    auxx, auxz, auxg, phiq, phik, run_col, den,
    s_ax, r_ax, s_az, r_az, s_ag, r_ag,
    s_x, r_x, s_z, r_z, s_g, r_g, s_w, r_w, s_v, r_v,
):
    g = lax.axis_index("grp")
    s = lax.axis_index("seq")
    z, x = s // NX, s % NX

    def at_x(i):
        return (g, z * NX + i)

    def at_z(i):
        return (g, i * NX + x)

    def at_g(i):
        return (i, s)

    def copy(src, dst, ssem, rsem, to):
        return pltpu.make_async_remote_copy(
            src_ref=src, dst_ref=dst, send_sem=ssem, recv_sem=rsem, device_id=to, device_id_type=MESH
        )

    other_x = [(x + d) % NX for d in (2, 1, 3)]
    other_z = [(z + d) % NZ for d in (4, 3, 5, 2, 6, 1, 7)]
    other_g = [(g + d) % NG for d in (4, 3, 5, 2, 6, 1, 7)]

    barrier = pltpu.get_barrier_semaphore()
    for to in [at_x(i) for i in other_x] + [at_z(i) for i in other_z] + [at_g(i) for i in other_g]:
        pl.semaphore_signal(barrier, inc=1, device_id=to, device_id_type=MESH)

    lane = lax.broadcasted_iota(jnp.int32, (HEADS, T), 1)
    running = rate_ref[...]
    step = 1
    while step < T:
        running = running + jnp.where(lane >= step, pltpu.roll(running, step, 1), 0.0)
        step *= 2
    total = jnp.broadcast_to(running[:, T - 1 : T], (HEADS, T))
    columns = running.T
    fade = jnp.exp(-(total - running)).T
    run_col[...] = columns

    for h in range(HEADS):
        at = pl.ds(h * T, T)
        w = wk_ref[h]
        phi = softplus(dot(k_ref[:, at], jnp.concatenate([w, -w], axis=-1))).astype(BF16)
        phik[h] = phi
        faded = phi.astype(F32) * fade[:, h : h + 1]
        auxx[x, pl.ds(h, 1), :] = jnp.sum(faded, axis=0, keepdims=True)
        own[at, :] = dot(faded.astype(BF16), v_ref[:, at], ((0,), (0,)))
    auxx[x, pl.ds(HEADS, HEADS), :] = jnp.exp(-total)
    quarter = HEADS * T // NX
    xin[x] = own[pl.ds(pl.multiple_of(x * quarter, quarter), quarter), :].reshape(NZ, SLICE, T)

    pl.semaphore_wait(barrier, len(other_x) + len(other_z) + len(other_g))

    sent = []

    def send(*args):
        c = copy(*args)
        c.start()
        sent.append(c)

    for n, i in enumerate(other_x):
        send(auxx.at[x], auxx.at[x], s_ax.at[n], r_ax.at[x], at_x(i))
    order = other_z + [z]
    for m, c in enumerate(order):
        for n, i in enumerate(other_x):
            row = pl.multiple_of(i * quarter + c * SLICE, SLICE)
            send(own.at[pl.ds(row, SLICE)], xin.at[x, c], s_x.at[n * NZ + m], r_x.at[x * NZ + c], at_x(i))

    causal = lax.broadcasted_iota(jnp.int32, (T, T), 0) >= lax.broadcasted_iota(jnp.int32, (T, T), 1)

    def attend(h):
        at = pl.ds(h * T, T)
        w = wq_ref[h]
        phi = softplus(dot(q_ref[:, at], jnp.concatenate([w, -w], axis=-1))).astype(BF16)
        phiq[h] = phi
        scores = dot(phi, phik[h], ((1,), (1,)))
        spacing = columns[:, h : h + 1] - running[h : h + 1, :]
        weighted = jnp.where(causal, scores * jnp.exp(-spacing), 0.0)
        den[:, h : h + 1] = jnp.sum(weighted, axis=1, keepdims=True)
        o_ref[:, at] = dot(weighted.astype(BF16), v_ref[:, at])

    for h in range(0, 2):
        attend(h)

    for i in other_x:
        copy(auxx.at[x], auxx.at[i], s_ax.at[0], r_ax.at[i], at_x(i)).wait_recv()
    zero = jnp.zeros((HEADS, T), F32)
    one = jnp.ones((HEADS, T), F32)

    def chain(aux, n, here):
        norm, decay, norm_before, decay_before = zero, one, zero, one
        for i in range(n):
            norm_before = jnp.where(here == i, norm, norm_before)
            decay_before = jnp.where(here == i, decay, decay_before)
            d = aux[i, pl.ds(HEADS, HEADS), :]
            norm = d * norm + aux[i, pl.ds(0, HEADS), :]
            decay = d * decay
        return norm, decay, norm_before, decay_before

    norm, decay, norm_x, decay_x = chain(auxx, NX, x)
    auxz[z, pl.ds(0, HEADS), :] = norm
    auxz[z, pl.ds(HEADS, HEADS), :] = decay
    for n, i in enumerate(other_z):
        send(auxz.at[z], auxz.at[z], s_az.at[n], r_az.at[z], at_z(i))

    def head_row(aux, i, c):
        head = (x * NZ + c) // PER_HEAD
        return aux[i, pl.ds(HEADS + head, 1), :]

    for n, c in enumerate(order):
        for i in other_x:
            copy(own.at[pl.ds(0, SLICE)], xin.at[i, c], s_x.at[0], r_x.at[i * NZ + c], at_x(i)).wait_recv()
        acc = xin[0, c]
        for i in range(1, NX):
            acc = head_row(auxx, i, c) * acc + xin[i, c]
        if n < NZ - 1:
            tout[n] = acc
            send(tout.at[n], zin.at[z], s_z.at[n], r_z.at[z], at_z(c))
        else:
            zin[z] = acc

    for h in range(2, 5):
        attend(h)

    for i in other_z:
        copy(auxz.at[z], auxz.at[i], s_az.at[0], r_az.at[i], at_z(i)).wait_recv()
    norm, decay, norm_z, decay_z = chain(auxz, NZ, z)
    auxg[g, pl.ds(0, HEADS), :] = norm
    auxg[g, pl.ds(HEADS, HEADS), :] = decay
    for n, i in enumerate(other_g):
        send(auxg.at[g], auxg.at[g], s_ag.at[n], r_ag.at[g], at_g(i))
    for i in other_z:
        copy(tout.at[0], zin.at[i], s_z.at[0], r_z.at[i], at_z(i)).wait_recv()
    acc = zin[0]
    for i in range(1, NZ):
        acc = head_row(auxz, i, z) * acc + zin[i]
    gin[g] = acc
    for n, i in enumerate(other_g):
        send(gin.at[g], gin.at[g], s_g.at[n], r_g.at[g], at_g(i))

    for h in range(5, 8):
        attend(h)

    for i in other_g:
        copy(auxg.at[g], auxg.at[i], s_ag.at[0], r_ag.at[i], at_g(i)).wait_recv()
    for i in other_g:
        copy(gin.at[g], gin.at[i], s_g.at[0], r_g.at[i], at_g(i)).wait_recv()
    acc = jnp.zeros((SLICE, T), F32)
    for i in range(NG - 1):
        acc = jnp.where(i < g, head_row(auxg, i, z) * acc + gin[i], acc)
    for i in range(NZ):
        wout[i] = acc
        if i < NZ - 1:
            acc = head_row(auxz, i, z) * acc + zin[i]
    cin[z] = wout[z]
    for n, i in enumerate(other_z):
        send(wout.at[i], cin.at[z], s_w.at[n], r_w.at[z], at_z(i))

    _, _, norm_g, _ = chain(auxg, NG, g)
    norm_in = decay_x * (decay_z * norm_g + norm_z) + norm_x
    lead = jnp.exp(-columns)
    for h in range(HEADS):
        at = pl.ds(h * T, T)
        from_norm = jnp.sum(phiq[h].astype(F32) * norm_in[h : h + 1, :], axis=1, keepdims=True)
        inverse = 1.0 / (den[:, h : h + 1] + lead[:, h : h + 1] * from_norm)
        o_ref[:, at] = o_ref[:, at] * inverse - t_ref[:, at].astype(F32)
        den[:, h : h + 1] = lead[:, h : h + 1] * inverse

    for m, c in enumerate([z] + other_z[::-1]):
        if m:
            copy(wout.at[0], cin.at[c], s_w.at[0], r_w.at[c], at_z(c)).wait_recv()
        acc = cin[c]
        for i in range(NX):
            vout[i, c] = acc
            if i < NX - 1:
                acc = head_row(auxx, i, c) * acc + xin[i, c]
        for n, i in enumerate(other_x):
            send(vout.at[i, c], fin.at[x, c], s_v.at[n * NZ + m], r_v.at[x * NZ + c], at_x(i))
    fin[x] = vout[x]

    per_x = HEADS // NX
    for h in range(HEADS):
        at = pl.ds(h * T, T)
        owner, first = h // per_x, (h % per_x) * PER_HEAD

        @pl.when(owner != x)
        def _():
            for c in range(first, first + PER_HEAD):
                copy(vout.at[0, 0], fin.at[owner, c], s_v.at[0], r_v.at[owner * NZ + c], at_x(owner)).wait_recv()

        state = fin[owner, pl.ds(first, PER_HEAD)].reshape(T, T)
        high = state.astype(BF16)
        low = (state - high.astype(F32)).astype(BF16)
        phi = phiq[h]
        o_ref[:, at] = o_ref[:, at] + den[:, h : h + 1] * (dot(phi, high) + dot(phi, low))

    for c in sent:
        c.wait_send()


def local(query_rows, key_rows, value_rows, teacher, query_map, key_map, decay_rate):
    shape = query_rows.shape[1:]
    vmem = pl.BlockSpec(memory_space=pltpu.VMEM)
    dma = lambda n: pltpu.SemaphoreType.DMA((n,))
    part = lambda *lead: pltpu.VMEM(lead + (SLICE, T), F32)
    aux = lambda n: pltpu.VMEM((n, 2 * HEADS, T), F32)
    out = pl.pallas_call(
        kernel,
        out_shape=jax.ShapeDtypeStruct(shape, F32),
        in_specs=[vmem] * 7,
        out_specs=vmem,
        scratch_shapes=[
            pltpu.VMEM((HEADS * T, T), F32),
            part(NX, NZ),
            part(NZ - 1),
            part(NZ),
            part(NG),
            part(NZ),
            part(NZ),
            part(NX, NZ),
            part(NX, NZ),
            aux(NX),
            aux(NZ),
            aux(NG),
            pltpu.VMEM((HEADS, T, T), BF16),
            pltpu.VMEM((HEADS, T, T), BF16),
            pltpu.VMEM((T, HEADS), F32),
            pltpu.VMEM((T, HEADS), F32),
            dma(NX - 1), dma(NX), dma(NZ - 1), dma(NZ), dma(NG - 1), dma(NG),
            dma((NX - 1) * NZ), dma(NX * NZ), dma(NZ - 1), dma(NZ), dma(NG - 1), dma(NG),
            dma(NZ - 1), dma(NZ), dma((NX - 1) * NZ), dma(NX * NZ),
        ],
        compiler_params=pltpu.CompilerParams(
            collective_id=0, has_side_effects=True, vmem_limit_bytes=32 * 1024 * 1024
        ),
    )(
        query_rows.reshape(shape),
        key_rows.reshape(shape),
        value_rows.reshape(shape),
        teacher.reshape(shape),
        query_map,
        key_map,
        decay_rate.reshape(decay_rate.shape[1:]),
    )
    return out.reshape(query_rows.shape)


def solution(mesh):
    rows = P(None, ("grp", "seq"), None)
    return jax.shard_map(
        local,
        mesh=mesh,
        in_specs=(rows, rows, rows, rows, P(), P(), P(None, None, ("grp", "seq"))),
        out_specs=rows,
        check_vma=False,
    )
```

```python
import jax
import jax.numpy as jnp
from jax import lax
from jax.experimental import pallas as pl
from jax.experimental.pallas import tpu as pltpu
from jax.sharding import PartitionSpec as P

MESH = pl.DeviceIdType.MESH
F32 = jnp.float32
BF16 = jnp.bfloat16

NX, NZ, NG = 4, 8, 8
HEADS = 8
T = 128
SLICE = HEADS * T // (NX * NZ)
PER_HEAD = T // SLICE
PER_X = HEADS // NX
ROW = pl.ds(0, HEADS)
DECAY = pl.ds(HEADS, HEADS)


def dot(a, b, dims=((1,), (0,))):
    return lax.dot_general(a, b, (dims, ((), ())), preferred_element_type=F32)


def lanes(h):
    return pl.ds(h * T, T) if isinstance(h, int) else pl.ds(pl.multiple_of(h * T, T), T)


def kernel(
    q_hbm, k_hbm, v_hbm, t_hbm, wq_hbm, wk_hbm, rate_hbm, o_ref,
    q_ref, k_ref, v_ref, t_ref, wq_ref, wk_ref, rate_ref,
    own, xin, before, term, tout, zin, gin, wout, cin, fin,
    dx, nx, auxz, auxg, phiq, phik, run, run_col, den,
    s_in, s_dx, r_dx, s_nx, r_nx, s_az, r_az, s_ag, r_ag,
    s_x, r_x, s_z, r_z, s_g, r_g, s_w, r_w, s_v, r_v, s_t, r_t,
):
    g = lax.axis_index("grp")
    s = lax.axis_index("seq")
    z, x = s // NX, s % NX

    def at_x(i):
        return (g, z * NX + i)

    def at_z(i):
        return (g, i * NX + x)

    def at_g(i):
        return (i, s)

    def copy(src, dst, ssem, rsem, to):
        return pltpu.make_async_remote_copy(
            src_ref=src, dst_ref=dst, send_sem=ssem, recv_sem=rsem, device_id=to, device_id_type=MESH
        )

    other_x = [(x + d) % NX for d in (2, 1, 3)]
    other_z = [(z + d) % NZ for d in (4, 3, 5, 2, 6, 1, 7)]
    order = other_z + [z]
    other_g = [(g + d) % NG for d in (4, 3, 5, 2, 6, 1, 7)]

    barrier = pltpu.get_barrier_semaphore()
    for to in [at_z(i) for i in other_z] + [at_g(i) for i in other_g] + [at_x(i) for i in other_x]:
        pl.semaphore_signal(barrier, inc=1, device_id=to, device_id_type=MESH)

    pairs = [
        (rate_hbm, rate_ref), (wk_hbm, wk_ref), (k_hbm, k_ref), (v_hbm, v_ref),
        (wq_hbm, wq_ref), (q_hbm, q_ref), (t_hbm, t_ref),
    ]
    loads = [pltpu.make_async_copy(a, b, s_in.at[n]) for n, (a, b) in enumerate(pairs)]
    for load in loads:
        load.start()

    sent = []

    def send(*args):
        c = copy(*args)
        c.start()
        sent.append(c)

    loads[0].wait()
    lane = lax.broadcasted_iota(jnp.int32, (HEADS, T), 1)
    running = rate_ref[...]
    step = 1
    while step < T:
        running = running + jnp.where(lane >= step, pltpu.roll(running, step, 1), 0.0)
        step *= 2
    total = jnp.broadcast_to(running[:, T - 1 : T], (HEADS, T))
    run[ROW, :] = running
    run[DECAY, :] = jnp.exp(running - total)
    dx[x] = jnp.exp(-total)

    half = NZ // 2

    def states(e):
        for p in range(NX):
            h = PER_X * p + e
            product = dot(wk_ref[h], k_ref[:, lanes(h)], ((1,), (1,)))
            both = jnp.log1p(jnp.exp(-jnp.abs(product)))
            phi = jnp.concatenate([jnp.maximum(product, 0.0) + both, jnp.maximum(-product, 0.0) + both], axis=0)
            phi = phi.astype(BF16)
            phik[h] = phi
            faded = phi.astype(F32) * run[pl.ds(HEADS + h, 1), :]
            own[p, pl.ds(e * half, half)] = dot(faded.astype(BF16), v_ref[:, lanes(h)]).reshape(half, SLICE, T)

    def send_slices(m0, slots):
        for m, c in enumerate(slots):
            for n, i in enumerate(other_x):
                send(own.at[i, c], xin.at[x, c], s_x.at[n * NZ + m0 + m], r_x.at[x * NZ + c], at_x(i))

    loads[1].wait()
    loads[2].wait()
    loads[3].wait()
    states(0)
    states(1)
    for h in range(HEADS):
        fade = run[pl.ds(HEADS + h, 1), :]
        high = fade.astype(BF16)
        low = (fade - high.astype(F32)).astype(BF16)
        sums = dot(jnp.concatenate([high, low], axis=0), phik[h], ((1,), (1,)))
        nx[x, pl.ds(h, 1), :] = sums[0:1, :] + sums[1:2, :]
    pl.semaphore_wait(barrier, len(other_x) + len(other_z) + len(other_g))
    for n, i in enumerate(other_x):
        send(dx.at[x], dx.at[x], s_dx.at[n], r_dx.at[x], at_x(i))
    send_slices(0, order[:half])
    for n, i in enumerate(other_x):
        send(nx.at[x], nx.at[x], s_nx.at[n], r_nx.at[x], at_x(i))
    send_slices(half, order[half:])
    xin[x] = own[x]

    causal = lax.broadcasted_iota(jnp.int32, (T, T), 0) >= lax.broadcasted_iota(jnp.int32, (T, T), 1)
    loads[4].wait()
    loads[5].wait()
    loads[6].wait()
    for h in range(HEADS):
        w = wq_ref[h]
        product = dot(q_ref[:, lanes(h)], jnp.concatenate([w, -w], axis=0), ((1,), (1,)))
        phi = (jnp.maximum(product, 0.0) + jnp.log1p(jnp.exp(-jnp.abs(product)))).astype(BF16)
        phiq[h] = phi
        column = jnp.broadcast_to(run[pl.ds(h, 1), :], (T, T)).T
        run_col[h] = column
        scores = dot(phi, phik[h])
        weighted = jnp.where(causal, scores * jnp.exp(run[pl.ds(h, 1), :] - column), 0.0)
        den[h] = jnp.broadcast_to(jnp.sum(weighted, axis=1, keepdims=True), (T, T))
        o_ref[:, lanes(h)] = dot(weighted.astype(BF16), v_ref[:, lanes(h)])

    def head_row(ref, i, c, first):
        return ref[i, pl.ds(first + (x * NZ + c) // PER_HEAD, 1), :]

    def row_totals(m0, slots):
        for m, c in enumerate(slots):
            for i in other_x:
                copy(own.at[0, 0], xin.at[i, c], s_x.at[0], r_x.at[i * NZ + c], at_x(i)).wait_recv()
            acc = jnp.zeros((SLICE, T), F32)
            for i in range(NX):
                before[i, c] = acc
                acc = head_row(dx, i, c, 0) * acc + xin[i, c]
            if m0 + m < NZ - 1:
                tout[m0 + m] = acc
                send(tout.at[m0 + m], zin.at[z], s_z.at[m0 + m], r_z.at[z], at_z(c))
            else:
                zin[z] = acc

    for i in other_x:
        copy(dx.at[x], dx.at[i], s_dx.at[0], r_dx.at[i], at_x(i)).wait_recv()
    row_totals(0, order[:half])

    def chain(parts, here):
        norm, decay = jnp.zeros((HEADS, T), F32), jnp.ones((HEADS, T), F32)
        norm_before, decay_before = norm, decay
        for i, (n, d) in enumerate(parts):
            norm_before = jnp.where(here == i, norm, norm_before)
            decay_before = jnp.where(here == i, decay, decay_before)
            norm = d * norm + n
            decay = d * decay
        return norm, decay, norm_before, decay_before

    for i in other_x:
        copy(nx.at[x], nx.at[i], s_nx.at[0], r_nx.at[i], at_x(i)).wait_recv()
    norm, decay, norm_x, decay_x = chain([(nx[i], dx[i]) for i in range(NX)], x)
    auxz[z, ROW, :] = norm
    auxz[z, DECAY, :] = decay
    for n, i in enumerate(other_z):
        send(auxz.at[z], auxz.at[z], s_az.at[n], r_az.at[z], at_z(i))
    row_totals(half, order[half:])
    for n, i in enumerate(other_x):
        send(before.at[i], term.at[x], s_t.at[n], r_t.at[x], at_x(i))

    for i in other_z:
        copy(auxz.at[z], auxz.at[i], s_az.at[0], r_az.at[i], at_z(i)).wait_recv()
    norm, decay, norm_z, decay_z = chain([(auxz[i, ROW, :], auxz[i, DECAY, :]) for i in range(NZ)], z)
    auxg[g, ROW, :] = norm
    auxg[g, DECAY, :] = decay

    def each_later(act):
        for i in range(1, NG):
            @pl.when(i > g)
            def _(i=i):
                act(i)

    def each_earlier(act):
        for i in range(NG - 1):
            @pl.when(i < g)
            def _(i=i):
                act(i)

    def aux_to(i):
        return copy(auxg.at[g], auxg.at[g], s_ag.at[i], r_ag.at[g], at_g(i))

    def total_to(i):
        return copy(gin.at[g], gin.at[g], s_g.at[i], r_g.at[g], at_g(i))

    each_later(lambda i: aux_to(i).start())
    for i in other_z:
        copy(tout.at[0], zin.at[i], s_z.at[0], r_z.at[i], at_z(i)).wait_recv()
    acc = zin[0]
    for i in range(1, NZ):
        acc = head_row(auxz, i, z, HEADS) * acc + zin[i]
    gin[g] = acc
    each_later(lambda i: total_to(i).start())

    each_earlier(lambda i: copy(auxg.at[g], auxg.at[i], s_ag.at[0], r_ag.at[i], at_g(i)).wait_recv())
    each_earlier(lambda i: copy(gin.at[g], gin.at[i], s_g.at[0], r_g.at[i], at_g(i)).wait_recv())
    acc = jnp.zeros((SLICE, T), F32)
    for i in range(NG - 1):
        acc = jnp.where(i < g, head_row(auxg, i, z, HEADS) * acc + gin[i], acc)

    def carry_to(i):
        return copy(wout.at[i], cin.at[z], s_w.at[i], r_w.at[z], at_z(i))

    for i in range(NZ):
        wout[i] = acc

        @pl.when(i != z)
        def _(i=i):
            carry_to(i).start()

        if i < NZ - 1:
            acc = head_row(auxz, i, z, HEADS) * acc + zin[i]
    cin[z] = wout[z]

    norm_g = jnp.zeros((HEADS, T), F32)
    for i in range(NG - 1):
        norm_g = jnp.where(i < g, auxg[i, DECAY, :] * norm_g + auxg[i, ROW, :], norm_g)
    norm_in = decay_x * (decay_z * norm_g + norm_z) + norm_x
    for h in range(HEADS):
        lead = jnp.exp(-run_col[h])
        from_norm = jnp.sum(phiq[h].astype(F32) * norm_in[h : h + 1, :], axis=1, keepdims=True)
        inverse = 1.0 / (den[h] + lead * from_norm)
        o_ref[:, lanes(h)] = o_ref[:, lanes(h)] * inverse - t_ref[:, lanes(h)].astype(F32)
        den[h] = lead * inverse

    for m, c in enumerate([z] + other_z[::-1]):
        if m:
            copy(wout.at[0], cin.at[c], s_w.at[0], r_w.at[c], at_z(c)).wait_recv()
        for n, i in enumerate(other_x):
            send(cin.at[c], fin.at[x, c], s_v.at[n * NZ + m], r_v.at[x * NZ + c], at_x(i))

    def finish(p, carry, row_term):
        for e in range(PER_X):
            h = PER_X * p + e
            part = pl.ds(e * PER_HEAD, PER_HEAD)
            state = run[pl.ds(h, 1), :] * carry[part].reshape(T, T) + row_term[part].reshape(T, T)
            high = state.astype(BF16)
            low = (state - high.astype(F32)).astype(BF16)
            phi = phiq[h]
            o_ref[:, lanes(h)] = o_ref[:, lanes(h)] + den[h] * (dot(phi, high) + dot(phi, low))

    run[ROW, :] = decay_x
    for i in other_x:
        copy(before.at[0], term.at[i], s_t.at[0], r_t.at[i], at_x(i)).wait_recv()
    finish(x, cin, before.at[x])
    for p in other_x[::-1]:
        for c in range(NZ):
            copy(cin.at[0], fin.at[p, c], s_v.at[0], r_v.at[p * NZ + c], at_x(p)).wait_recv()
        finish(p, fin.at[p], term.at[p])

    for c in sent:
        c.wait_send()
    each_later(lambda i: aux_to(i).wait_send())
    each_later(lambda i: total_to(i).wait_send())
    for i in range(NZ):
        @pl.when(i != z)
        def _(i=i):
            carry_to(i).wait_send()


def local(query_rows, key_rows, value_rows, teacher, query_map, key_map, decay_rate):
    rows = query_rows.shape[1:]
    operands = (
        query_rows.reshape(rows),
        key_rows.reshape(rows),
        value_rows.reshape(rows),
        teacher.reshape(rows),
        jnp.swapaxes(query_map, 1, 2),
        jnp.swapaxes(key_map, 1, 2),
        decay_rate.reshape(decay_rate.shape[1:]),
    )
    dma = lambda n: pltpu.SemaphoreType.DMA((n,))
    part = lambda *lead: pltpu.VMEM(lead + (SLICE, T), F32)
    small = lambda *lead: pltpu.VMEM(lead + (T,), F32)
    out = pl.pallas_call(
        kernel,
        out_shape=jax.ShapeDtypeStruct(rows, F32),
        in_specs=[pl.BlockSpec(memory_space=pltpu.HBM)] * 7,
        out_specs=pl.BlockSpec(memory_space=pltpu.VMEM),
        scratch_shapes=[pltpu.VMEM(a.shape, a.dtype) for a in operands]
        + [
            part(NX, NZ), part(NX, NZ), part(NX, NZ), part(NX, NZ), part(NZ - 1), part(NZ), part(NG),
            part(NZ), part(NZ), part(NX, NZ),
            small(NX, HEADS), small(NX, HEADS), small(NZ, 2 * HEADS), small(NG, 2 * HEADS),
            pltpu.VMEM((HEADS, T, T), BF16), pltpu.VMEM((HEADS, T, T), BF16),
            small(2 * HEADS), small(HEADS, T), small(HEADS, T),
            dma(7), dma(NX - 1), dma(NX), dma(NX - 1), dma(NX), dma(NZ - 1), dma(NZ), dma(NG), dma(NG),
            dma((NX - 1) * NZ), dma(NX * NZ), dma(NZ - 1), dma(NZ), dma(NG), dma(NG),
            dma(NZ), dma(NZ), dma((NX - 1) * NZ), dma(NX * NZ), dma(NX - 1), dma(NX),
        ],
        compiler_params=pltpu.CompilerParams(
            collective_id=0, has_side_effects=True, vmem_limit_bytes=32 * 1024 * 1024
        ),
    )(*[pltpu.with_memory_space_constraint(a, pltpu.HBM) for a in operands])
    return out.reshape(query_rows.shape)


def solution(mesh):
    rows = P(None, ("grp", "seq"), None)
    return jax.shard_map(
        local,
        mesh=mesh,
        in_specs=(rows, rows, rows, rows, P(), P(), P(None, None, ("grp", "seq"))),
        out_specs=rows,
        check_vma=False,
    )
```

```python
import jax
import jax.numpy as jnp
from jax import lax
from jax.experimental import pallas as pl
from jax.experimental.pallas import tpu as pltpu
from jax.sharding import PartitionSpec as P

MESH = pl.DeviceIdType.MESH
F32 = jnp.float32
BF16 = jnp.bfloat16

NX, NZ, NG = 4, 8, 8
HEADS = 8
T = 128
SLICE = HEADS * T // (NX * NZ)
PER_HEAD = T // SLICE
PER_X = HEADS // NX
AUX = 2 * HEADS
HALF = NZ // 2
SIDE = HALF * SLICE
QUARTER = 2 * SIDE + AUX


def dot(a, b, dims=((1,), (0,))):
    return lax.dot_general(a, b, (dims, ((), ())), preferred_element_type=F32)


def lanes(h):
    return pl.ds(h * T, T)


def slice_row(c):
    return c * SLICE + (c // HALF) * AUX


def kernel(
    q_hbm, k_hbm, v_hbm, t_hbm, wq_hbm, wk_hbm, rate_hbm, o_ref,
    q_ref, k_ref, v_ref, t_ref, wq_ref, wk_ref, rate_ref,
    own, xin, before, term, tout, zin, gin, wout, cin, fin,
    phiq, phik, run, run_col, den,
    s_in, s_x, r_x, s_z, r_z, s_g, r_g, s_w, r_w, s_v, r_v, s_t, r_t,
):
    g = lax.axis_index("grp")
    s = lax.axis_index("seq")
    z, x = s // NX, s % NX

    def at_x(i):
        return (g, z * NX + i)

    def at_z(i):
        return (g, i * NX + x)

    def at_g(i):
        return (i, s)

    def copy(src, dst, ssem, rsem, to):
        return pltpu.make_async_remote_copy(
            src_ref=src, dst_ref=dst, send_sem=ssem, recv_sem=rsem, device_id=to, device_id_type=MESH
        )

    other_x = [(x + d) % NX for d in (2, 1, 3)]
    other_z = [(z + d) % NZ for d in (4, 3, 5, 2, 6, 1, 7)]
    other_g = [(g + d) % NG for d in (4, 3, 5, 2, 6, 1, 7)]

    barrier = pltpu.get_barrier_semaphore()
    for to in [at_z(i) for i in other_z] + [at_g(i) for i in other_g] + [at_x(i) for i in other_x]:
        pl.semaphore_signal(barrier, inc=1, device_id=to, device_id_type=MESH)

    pairs = [
        (rate_hbm, rate_ref), (wk_hbm, wk_ref), (k_hbm, k_ref), (v_hbm, v_ref),
        (wq_hbm, wq_ref), (q_hbm, q_ref), (t_hbm, t_ref),
    ]
    loads = [pltpu.make_async_copy(a, b, s_in.at[n]) for n, (a, b) in enumerate(pairs)]
    for load in loads:
        load.start()

    loads[0].wait()
    lane = lax.broadcasted_iota(jnp.int32, (HEADS, T), 1)
    running = rate_ref[...]
    step = 1
    while step < T:
        running = running + jnp.where(lane >= step, pltpu.roll(running, step, 1), 0.0)
        step *= 2
    total = jnp.broadcast_to(running[:, T - 1 : T], (HEADS, T))
    run[pl.ds(0, HEADS), :] = running
    fades = jnp.exp(running - total)

    loads[1].wait()
    loads[2].wait()
    loads[3].wait()
    sums = []
    for h in range(HEADS):
        product = dot(wk_ref[h], k_ref[:, lanes(h)], ((1,), (1,)))
        both = jnp.log1p(jnp.exp(-jnp.abs(product)))
        phi = jnp.concatenate([jnp.maximum(product, 0.0) + both, jnp.maximum(-product, 0.0) + both], axis=0)
        phi = phi.astype(BF16)
        phik[h] = phi
        fade = fades[h : h + 1, :]
        faded = phi.astype(F32) * fade
        at = slice_row((h % PER_X) * PER_HEAD)
        own[h // PER_X, pl.ds(at, T), :] = dot(faded.astype(BF16), v_ref[:, lanes(h)])
        high = fade.astype(BF16)
        low = (fade - high.astype(F32)).astype(BF16)
        pair = dot(jnp.concatenate([high, low], axis=0), phi, ((1,), (1,)))
        sums.append(pair[0:1, :] + pair[1:2, :])
    aux = jnp.concatenate(sums + [jnp.exp(-total)], axis=0)
    for p in range(NX):
        own[p, pl.ds(SIDE, AUX), :] = aux

    pl.semaphore_wait(barrier, len(other_x) + len(other_z) + len(other_g))

    order = other_z + [z]

    def aux_to(i):
        at = pl.ds(SIDE, AUX)
        return copy(own.at[i, at], xin.at[x, at], s_x.at[0], r_x.at[NZ], at_x(i))

    def slice_at(c):
        return pl.ds(pl.multiple_of(slice_row(c), AUX), SLICE)

    def slice_to(i, c):
        at = slice_at(c)
        return copy(own.at[i, at], xin.at[x, at], s_x.at[0], r_x.at[c], at_x(i))

    for i in other_x:
        aux_to(i).start()
    for c in order:
        for i in other_x:
            slice_to(i, c).start()
    xin[x] = own[x]

    causal = lax.broadcasted_iota(jnp.int32, (T, T), 0) >= lax.broadcasted_iota(jnp.int32, (T, T), 1)

    def attend(start, end):
        for h in range(start, end):
            w = wq_ref[h]
            product = dot(q_ref[:, lanes(h)], jnp.concatenate([w, -w], axis=0), ((1,), (1,)))
            phi = (jnp.maximum(product, 0.0) + jnp.log1p(jnp.exp(-jnp.abs(product)))).astype(BF16)
            phiq[h] = phi
            row = run[pl.ds(h, 1), :]
            column = jnp.broadcast_to(row, (T, T)).T
            run_col[h] = column
            scores = dot(phi, phik[h])
            weighted = jnp.where(causal, scores * jnp.exp(row - column), 0.0)
            den[h] = jnp.broadcast_to(jnp.sum(weighted, axis=1, keepdims=True), (T, T))
            o_ref[:, lanes(h)] = dot(weighted.astype(BF16), v_ref[:, lanes(h)])

    loads[4].wait()
    loads[5].wait()
    loads[6].wait()
    attend(0, 4)

    def chain(ref, n, here, base):
        norm, decay = jnp.zeros((HEADS, T), F32), jnp.ones((HEADS, T), F32)
        norm_before, decay_before = norm, decay
        for i in range(n):
            norm_before = jnp.where(here == i, norm, norm_before)
            decay_before = jnp.where(here == i, decay, decay_before)
            d = ref[i, pl.ds(base + HEADS, HEADS), :]
            norm = d * norm + ref[i, pl.ds(base, HEADS), :]
            decay = d * decay
        return norm, decay, norm_before, decay_before

    def head_row(ref, i, base, c):
        return ref[i, pl.ds(base + HEADS + (x * NZ + c) // PER_HEAD, 1), :]

    def total_to_row(c):
        return copy(tout.at[c], zin.at[z], s_z.at[0], r_z.at[0], at_z(c))

    three = pl.ds(0, NX - 1)
    at = pl.ds(SIDE, AUX)
    copy(own.at[three, at], xin.at[three, at], s_x.at[0], r_x.at[NZ], at_x(other_x[0])).wait_recv()
    norm, decay, norm_x, decay_x = chain(xin, NX, x, SIDE)
    for c in order:
        at = slice_at(c)
        copy(own.at[three, at], xin.at[three, at], s_x.at[0], r_x.at[c], at_x(other_x[0])).wait_recv()
        acc = jnp.zeros((SLICE, T), F32)
        for i in range(NX):
            before[i, c] = acc
            acc = head_row(xin, i, SIDE, c) * acc + xin[i, at]
        tout[c, pl.ds(0, SLICE), :] = acc
        tout[c, pl.ds(SLICE, HEADS), :] = norm
        tout[c, pl.ds(SLICE + HEADS, HEADS), :] = decay

        @pl.when(c != z)
        def _(c=c):
            total_to_row(c).start()

    zin[z] = tout[z]
    for i in other_x:
        copy(before.at[i], term.at[x], s_t.at[0], r_t.at[0], at_x(i)).start()
    attend(4, 6)

    def each_later(act):
        for d in (4, 5, 3, 2, 6, 1, 7):
            @pl.when(g + d < NG)
            def _(d=d):
                act(g + d)

    def each_earlier(act):
        for i in range(NG - 1):
            @pl.when(i < g)
            def _(i=i):
                act(i)

    def total_to(i):
        return copy(gin.at[g], gin.at[g], s_g.at[i], r_g.at[g], at_g(i))

    seven = pl.ds(0, NZ - 1)
    copy(tout.at[seven], zin.at[seven], s_z.at[0], r_z.at[0], at_z(other_z[0])).wait_recv()
    acc = zin[0, pl.ds(0, SLICE), :]
    for i in range(1, NZ):
        acc = head_row(zin, i, SLICE, z) * acc + zin[i, pl.ds(0, SLICE), :]
    norm, decay, norm_z, decay_z = chain(zin, NZ, z, SLICE)
    gin[g, pl.ds(0, SLICE), :] = acc
    gin[g, pl.ds(SLICE, HEADS), :] = norm
    gin[g, pl.ds(SLICE + HEADS, HEADS), :] = decay
    each_later(lambda i: total_to(i).start())
    attend(6, HEADS)

    each_earlier(lambda i: copy(gin.at[g], gin.at[i], s_g.at[0], r_g.at[i], at_g(i)).wait_recv())
    acc = jnp.zeros((SLICE, T), F32)
    for i in range(NG - 1):
        acc = jnp.where(i < g, head_row(gin, i, SLICE, z) * acc + gin[i, pl.ds(0, SLICE), :], acc)

    def carry_to(i):
        return copy(wout.at[i], cin.at[z], s_w.at[0], r_w.at[z], at_z(i))

    for i in range(NZ):
        wout[i] = acc

        @pl.when(i != z)
        def _(i=i):
            carry_to(i).start()

        if i < NZ - 1:
            acc = head_row(zin, i, SLICE, z) * acc + zin[i, pl.ds(0, SLICE), :]
    cin[z] = wout[z]

    norm_g = jnp.zeros((HEADS, T), F32)
    for i in range(NG - 1):
        arrived = gin[i, pl.ds(SLICE + HEADS, HEADS), :] * norm_g + gin[i, pl.ds(SLICE, HEADS), :]
        norm_g = jnp.where(i < g, arrived, norm_g)
    norm_in = decay_x * (decay_z * norm_g + norm_z) + norm_x
    for h in range(HEADS):
        lead = jnp.exp(-run_col[h])
        from_norm = jnp.sum(phiq[h].astype(F32) * norm_in[h : h + 1, :], axis=1, keepdims=True)
        inverse = 1.0 / (den[h] + lead * from_norm)
        o_ref[:, lanes(h)] = o_ref[:, lanes(h)] * inverse - t_ref[:, lanes(h)].astype(F32)
        den[h] = lead * inverse
    run[pl.ds(HEADS, HEADS), :] = decay_x

    for m, c in enumerate([z] + other_z[::-1]):
        if m:
            copy(wout.at[0], cin.at[c], s_w.at[0], r_w.at[c], at_z(c)).wait_recv()
        for i in other_x:
            copy(cin.at[c], fin.at[x, c], s_v.at[0], r_v.at[x], at_x(i)).start()

    def finish(p, carry, row_term):
        for e in range(PER_X):
            h = PER_X * p + e
            part = pl.ds(e * PER_HEAD, PER_HEAD)
            state = run[pl.ds(HEADS + h, 1), :] * carry[part].reshape(T, T) + row_term[part].reshape(T, T)
            high = state.astype(BF16)
            low = (state - high.astype(F32)).astype(BF16)
            phi = phiq[h]
            at = pl.ds(pl.multiple_of(h * T, T), T)
            o_ref[:, at] = o_ref[:, at] + den[h] * (dot(phi, high) + dot(phi, low))

    copy(before.at[three], term.at[three], s_t.at[0], r_t.at[0], at_x(other_x[0])).wait_recv()
    finish(x, cin, before.at[x])
    for p in other_x[::-1]:
        copy(cin, fin.at[p], s_v.at[0], r_v.at[p], at_x(p)).wait_recv()
        finish(p, fin.at[p], term.at[p])

    to = at_x(other_x[0])
    copy(own.at[three], xin.at[three], s_x.at[0], r_x.at[0], to).wait_send()
    copy(before.at[three], term.at[three], s_t.at[0], r_t.at[0], to).wait_send()
    copy(fin.at[three], fin.at[three], s_v.at[0], r_v.at[0], to).wait_send()
    copy(tout.at[seven], zin.at[seven], s_z.at[0], r_z.at[0], at_z(other_z[0])).wait_send()
    copy(wout.at[seven], cin.at[seven], s_w.at[0], r_w.at[0], at_z(other_z[0])).wait_send()
    each_later(lambda i: total_to(i).wait_send())


def local(query_rows, key_rows, value_rows, teacher, query_map, key_map, decay_rate):
    rows = query_rows.shape[1:]
    operands = (
        query_rows.reshape(rows),
        key_rows.reshape(rows),
        value_rows.reshape(rows),
        teacher.reshape(rows),
        jnp.swapaxes(query_map, 1, 2),
        jnp.swapaxes(key_map, 1, 2),
        decay_rate.reshape(decay_rate.shape[1:]),
    )
    dma = lambda n: pltpu.SemaphoreType.DMA((n,))
    part = lambda *lead: pltpu.VMEM(lead + (SLICE, T), F32)
    rowed = lambda *lead: pltpu.VMEM(lead + (T,), F32)
    out = pl.pallas_call(
        kernel,
        out_shape=jax.ShapeDtypeStruct(rows, F32),
        in_specs=[pl.BlockSpec(memory_space=pltpu.HBM)] * 7,
        out_specs=pl.BlockSpec(memory_space=pltpu.VMEM),
        scratch_shapes=[pltpu.VMEM(a.shape, a.dtype) for a in operands]
        + [
            rowed(NX, QUARTER), rowed(NX, QUARTER), part(NX, NZ), part(NX, NZ),
            rowed(NZ, SLICE + AUX), rowed(NZ, SLICE + AUX), rowed(NG, SLICE + AUX),
            part(NZ), part(NZ), part(NX, NZ),
            pltpu.VMEM((HEADS, T, T), BF16), pltpu.VMEM((HEADS, T, T), BF16),
            rowed(2 * HEADS), rowed(HEADS, T), rowed(HEADS, T),
            dma(7), dma(1), dma(NZ + 1), dma(1), dma(1), dma(NG), dma(NG),
            dma(1), dma(NZ), dma(1), dma(NX), dma(1), dma(1),
        ],
        compiler_params=pltpu.CompilerParams(
            collective_id=0, has_side_effects=True, vmem_limit_bytes=32 * 1024 * 1024
        ),
    )(*[pltpu.with_memory_space_constraint(a, pltpu.HBM) for a in operands])
    return out.reshape(query_rows.shape)


def solution(mesh):
    rows = P(None, ("grp", "seq"), None)
    return jax.shard_map(
        local,
        mesh=mesh,
        in_specs=(rows, rows, rows, rows, P(), P(), P(None, None, ("grp", "seq"))),
        out_specs=rows,
        check_vma=False,
    )
```

```python
import jax
import jax.numpy as jnp
from jax import lax
from jax.experimental import pallas as pl
from jax.experimental.pallas import tpu as pltpu
from jax.sharding import PartitionSpec as P

MESH = pl.DeviceIdType.MESH
F32 = jnp.float32
BF16 = jnp.bfloat16

NX, NZ, NG = 4, 8, 8
HEADS = 8
T = 128
SLICE = HEADS * T // (NX * NZ)
PER_HEAD = T // SLICE
PER_X = HEADS // NX
AUX = 2 * HEADS
HALF = NZ // 2
SIDE = HALF * SLICE
QUARTER = 2 * SIDE + AUX


def dot(a, b, dims=((1,), (0,))):
    return lax.dot_general(a, b, (dims, ((), ())), preferred_element_type=F32)


def lanes(h):
    return pl.ds(h * T, T)


def slice_row(c):
    return c * SLICE + (c // HALF) * AUX


def kernel(
    q_hbm, k_hbm, v_hbm, t_hbm, wq_hbm, wk_hbm, rate_hbm, o_ref,
    q_ref, k_ref, v_ref, t_ref, wq_ref, wk_ref, rate_ref,
    own, xin, tout, zin, gin, auxz, auxg, wout, cin, vout, fin,
    phiq, phik, run, run_col, den,
    s_in, s_az, r_az, s_ag, r_ag, s_x, r_x, s_z, r_z, s_g, r_g, s_w, r_w, s_v, r_v,
):
    g = lax.axis_index("grp")
    s = lax.axis_index("seq")
    z, x = s // NX, s % NX

    def at_x(i):
        return (g, z * NX + i)

    def at_z(i):
        return (g, i * NX + x)

    def at_g(i):
        return (i, s)

    def copy(src, dst, ssem, rsem, to):
        return pltpu.make_async_remote_copy(
            src_ref=src, dst_ref=dst, send_sem=ssem, recv_sem=rsem, device_id=to, device_id_type=MESH
        )

    other_x = [(x + d) % NX for d in (2, 1, 3)]
    other_z = [(z + d) % NZ for d in (4, 3, 5, 2, 6, 1, 7)]
    other_g = [(g + d) % NG for d in (4, 3, 5, 2, 6, 1, 7)]

    barrier = pltpu.get_barrier_semaphore()
    for to in [at_z(i) for i in other_z] + [at_g(i) for i in other_g] + [at_x(i) for i in other_x]:
        pl.semaphore_signal(barrier, inc=1, device_id=to, device_id_type=MESH)

    pairs = [
        (rate_hbm, rate_ref), (wk_hbm, wk_ref), (k_hbm, k_ref), (v_hbm, v_ref),
        (wq_hbm, wq_ref), (q_hbm, q_ref), (t_hbm, t_ref),
    ]
    loads = [pltpu.make_async_copy(a, b, s_in.at[n]) for n, (a, b) in enumerate(pairs)]
    for load in loads:
        load.start()

    loads[0].wait()
    lane = lax.broadcasted_iota(jnp.int32, (HEADS, T), 1)
    running = rate_ref[...]
    step = 1
    while step < T:
        running = running + jnp.where(lane >= step, pltpu.roll(running, step, 1), 0.0)
        step *= 2
    total = jnp.broadcast_to(running[:, T - 1 : T], (HEADS, T))
    run[pl.ds(0, HEADS), :] = running
    fades = jnp.exp(running - total)

    loads[1].wait()
    loads[2].wait()
    loads[3].wait()
    sums = []
    for h in range(HEADS):
        product = dot(wk_ref[h], k_ref[:, lanes(h)], ((1,), (1,)))
        both = jnp.log1p(jnp.exp(-jnp.abs(product)))
        phi = jnp.concatenate([jnp.maximum(product, 0.0) + both, jnp.maximum(-product, 0.0) + both], axis=0)
        phi = phi.astype(BF16)
        phik[h] = phi
        fade = fades[h : h + 1, :]
        faded = phi.astype(F32) * fade
        at = slice_row((h % PER_X) * PER_HEAD)
        own[h // PER_X, pl.ds(at, T), :] = dot(faded.astype(BF16), v_ref[:, lanes(h)])
        high = fade.astype(BF16)
        low = (fade - high.astype(F32)).astype(BF16)
        pair = dot(jnp.concatenate([high, low], axis=0), phi, ((1,), (1,)))
        sums.append(pair[0:1, :] + pair[1:2, :])
    aux = jnp.concatenate(sums + [jnp.exp(-total)], axis=0)
    for p in range(NX):
        own[p, pl.ds(SIDE, AUX), :] = aux

    pl.semaphore_wait(barrier, len(other_x) + len(other_z) + len(other_g))

    odd = z % 2

    def slots(even_row, odd_row):
        return [(z + jnp.where(odd == 1, b, a)) % NZ for a, b in zip(even_row, odd_row)]

    order = slots((4, 2, 6, 0, 3, 5, 1, 7), (3, 5, 1, 7, 4, 2, 6, 0))

    def aux_to(i):
        at = pl.ds(SIDE, AUX)
        return copy(own.at[i, at], xin.at[x, at], s_x.at[0], r_x.at[NZ], at_x(i))

    def slice_at(c):
        return pl.ds(pl.multiple_of(slice_row(c), AUX), SLICE)

    def slice_to(i, c):
        at = slice_at(c)
        return copy(own.at[i, at], xin.at[x, at], s_x.at[0], r_x.at[c], at_x(i))

    for i in other_x:
        aux_to(i).start()
    for c in order:
        for i in other_x:
            slice_to(i, c).start()
    xin[x] = own[x]

    causal = lax.broadcasted_iota(jnp.int32, (T, T), 0) >= lax.broadcasted_iota(jnp.int32, (T, T), 1)

    def attend(start, end):
        for h in range(start, end):
            w = wq_ref[h]
            product = dot(q_ref[:, lanes(h)], jnp.concatenate([w, -w], axis=0), ((1,), (1,)))
            phi = (jnp.maximum(product, 0.0) + jnp.log1p(jnp.exp(-jnp.abs(product)))).astype(BF16)
            phiq[h] = phi
            row = run[pl.ds(h, 1), :]
            column = jnp.broadcast_to(row, (T, T)).T
            run_col[h] = column
            scores = dot(phi, phik[h])
            weighted = jnp.where(causal, scores * jnp.exp(row - column), 0.0)
            den[h] = jnp.broadcast_to(jnp.sum(weighted, axis=1, keepdims=True), (T, T))
            o_ref[:, lanes(h)] = dot(weighted.astype(BF16), v_ref[:, lanes(h)])

    loads[4].wait()
    loads[5].wait()
    loads[6].wait()
    attend(0, 4)

    def chain(ref, n, here, base):
        norm, decay = jnp.zeros((HEADS, T), F32), jnp.ones((HEADS, T), F32)
        norm_before, decay_before = norm, decay
        for i in range(n):
            norm_before = jnp.where(here == i, norm, norm_before)
            decay_before = jnp.where(here == i, decay, decay_before)
            d = ref[i, pl.ds(base + HEADS, HEADS), :]
            norm = d * norm + ref[i, pl.ds(base, HEADS), :]
            decay = d * decay
        return norm, decay, norm_before, decay_before

    def head_row(ref, i, base, c):
        return ref[i, pl.ds(base + HEADS + (x * NZ + c) // PER_HEAD, 1), :]

    def total_to_row(c):
        return copy(tout.at[c], zin.at[z], s_z.at[0], r_z.at[0], at_z(c))

    three = pl.ds(0, NX - 1)
    at = pl.ds(SIDE, AUX)
    copy(own.at[three, at], xin.at[three, at], s_x.at[0], r_x.at[NZ], at_x(other_x[0])).wait_recv()
    norm, decay, norm_x, decay_x = chain(xin, NX, x, SIDE)
    auxz[z, pl.ds(0, HEADS), :] = norm
    auxz[z, pl.ds(HEADS, HEADS), :] = decay
    for i in other_z:
        copy(auxz.at[z], auxz.at[z], s_az.at[0], r_az.at[0], at_z(i)).start()
    for c in order:
        at = slice_at(c)
        copy(own.at[three, at], xin.at[three, at], s_x.at[0], r_x.at[c], at_x(other_x[0])).wait_recv()
        acc = xin[0, at]
        for i in range(1, NX):
            acc = head_row(xin, i, SIDE, c) * acc + xin[i, at]
        tout[c] = acc

        @pl.when(c != z)
        def _(c=c):
            total_to_row(c).start()

    zin[z] = tout[z]
    attend(4, 6)

    def each_later(act):
        for d in (4, 5, 3, 2, 6, 1, 7):
            @pl.when(g + d < NG)
            def _(d=d):
                act(g + d)

    def each_earlier(act):
        for i in range(NG - 1):
            @pl.when(i < g)
            def _(i=i):
                act(i)

    def sums_to(i):
        return copy(auxg.at[g], auxg.at[g], s_ag.at[i], r_ag.at[g], at_g(i))

    def total_to(i):
        return copy(gin.at[g], gin.at[g], s_g.at[i], r_g.at[g], at_g(i))

    seven = pl.ds(0, NZ - 1)
    copy(auxz.at[seven], auxz.at[seven], s_az.at[0], r_az.at[0], at_z(other_z[0])).wait_recv()
    norm, decay, norm_z, decay_z = chain(auxz, NZ, z, 0)
    auxg[g, pl.ds(0, HEADS), :] = norm
    auxg[g, pl.ds(HEADS, HEADS), :] = decay
    each_later(lambda i: sums_to(i).start())
    copy(tout.at[seven], zin.at[seven], s_z.at[0], r_z.at[0], at_z(other_z[0])).wait_recv()
    acc = zin[0]
    for i in range(1, NZ):
        acc = head_row(auxz, i, 0, z) * acc + zin[i]
    gin[g] = acc
    each_later(lambda i: total_to(i).start())
    attend(6, HEADS)

    each_earlier(lambda i: copy(auxg.at[g], auxg.at[i], s_ag.at[i], r_ag.at[i], at_g(i)).wait_recv())
    each_earlier(lambda i: copy(gin.at[g], gin.at[i], s_g.at[i], r_g.at[i], at_g(i)).wait_recv())
    acc = jnp.zeros((SLICE, T), F32)
    for i in range(NG - 1):
        acc = jnp.where(i < g, head_row(auxg, i, 0, z) * acc + gin[i], acc)

    def carry_to(i):
        return copy(wout.at[i], cin.at[z], s_w.at[0], r_w.at[z], at_z(i))

    for i in range(NZ):
        wout[i] = acc
        if i < NZ - 1:
            acc = head_row(auxz, i, 0, z) * acc + zin[i]
    for d in (1, 7, 2, 6, 3, 5, 4):
        carry_to((z + d) % NZ).start()
    cin[z] = wout[z]

    norm_g = jnp.zeros((HEADS, T), F32)
    for i in range(NG - 1):
        arrived = auxg[i, pl.ds(HEADS, HEADS), :] * norm_g + auxg[i, pl.ds(0, HEADS), :]
        norm_g = jnp.where(i < g, arrived, norm_g)
    norm_in = decay_x * (decay_z * norm_g + norm_z) + norm_x
    for h in range(HEADS):
        lead = jnp.exp(-run_col[h])
        from_norm = jnp.sum(phiq[h].astype(F32) * norm_in[h : h + 1, :], axis=1, keepdims=True)
        inverse = 1.0 / (den[h] + lead * from_norm)
        o_ref[:, lanes(h)] = o_ref[:, lanes(h)] * inverse - t_ref[:, lanes(h)].astype(F32)
        den[h] = lead * inverse

    for c in slots((0, 2, 6, 4, 1, 7, 3, 5), (1, 7, 3, 5, 0, 2, 6, 4)):
        @pl.when(c != z)
        def _(c=c):
            copy(wout.at[0], cin.at[c], s_w.at[0], r_w.at[c], at_z(c)).wait_recv()

        at = slice_at(c)
        acc = cin[c]
        for i in range(NX):
            vout[i, c] = acc
            if i < NX - 1:
                acc = head_row(xin, i, SIDE, c) * acc + xin[i, at]
        for i in other_x:
            copy(vout.at[i, c], fin.at[x, c], s_v.at[0], r_v.at[x], at_x(i)).start()

    def finish(p, states):
        for e in range(PER_X):
            h = PER_X * p + e
            state = states[pl.ds(e * PER_HEAD, PER_HEAD)].reshape(T, T)
            high = state.astype(BF16)
            low = (state - high.astype(F32)).astype(BF16)
            phi = phiq[h]
            at = pl.ds(pl.multiple_of(h * T, T), T)
            o_ref[:, at] = o_ref[:, at] + den[h] * (dot(phi, high) + dot(phi, low))

    finish(x, vout.at[x])
    for p in other_x[::-1]:
        copy(vout.at[0], fin.at[p], s_v.at[0], r_v.at[p], at_x(p)).wait_recv()
        finish(p, fin.at[p])

    to = at_x(other_x[0])
    copy(own.at[three], xin.at[three], s_x.at[0], r_x.at[0], to).wait_send()
    copy(vout.at[three], fin.at[three], s_v.at[0], r_v.at[0], to).wait_send()
    copy(tout.at[seven], zin.at[seven], s_z.at[0], r_z.at[0], at_z(other_z[0])).wait_send()
    copy(wout.at[seven], cin.at[seven], s_w.at[0], r_w.at[0], at_z(other_z[0])).wait_send()
    each_later(lambda i: total_to(i).wait_send())
    each_later(lambda i: sums_to(i).wait_send())
    copy(auxz.at[seven], auxz.at[seven], s_az.at[0], r_az.at[0], at_z(other_z[0])).wait_send()


def local(query_rows, key_rows, value_rows, teacher, query_map, key_map, decay_rate):
    rows = query_rows.shape[1:]
    operands = (
        query_rows.reshape(rows),
        key_rows.reshape(rows),
        value_rows.reshape(rows),
        teacher.reshape(rows),
        jnp.swapaxes(query_map, 1, 2),
        jnp.swapaxes(key_map, 1, 2),
        decay_rate.reshape(decay_rate.shape[1:]),
    )
    dma = lambda n: pltpu.SemaphoreType.DMA((n,))
    part = lambda *lead: pltpu.VMEM(lead + (SLICE, T), F32)
    rowed = lambda *lead: pltpu.VMEM(lead + (T,), F32)
    out = pl.pallas_call(
        kernel,
        out_shape=jax.ShapeDtypeStruct(rows, F32),
        in_specs=[pl.BlockSpec(memory_space=pltpu.HBM)] * 7,
        out_specs=pl.BlockSpec(memory_space=pltpu.VMEM),
        scratch_shapes=[pltpu.VMEM(a.shape, a.dtype) for a in operands]
        + [
            rowed(NX, QUARTER), rowed(NX, QUARTER),
            part(NZ), part(NZ), part(NG), rowed(NZ, AUX), rowed(NG, AUX),
            part(NZ), part(NZ), part(NX, NZ), part(NX, NZ),
            pltpu.VMEM((HEADS, T, T), BF16), pltpu.VMEM((HEADS, T, T), BF16),
            rowed(HEADS), rowed(HEADS, T), rowed(HEADS, T),
            dma(7), dma(1), dma(1), dma(NG), dma(NG), dma(1), dma(NZ + 1), dma(1), dma(1), dma(NG), dma(NG),
            dma(1), dma(NZ), dma(1), dma(NX),
        ],
        compiler_params=pltpu.CompilerParams(
            collective_id=0, has_side_effects=True, vmem_limit_bytes=32 * 1024 * 1024
        ),
    )(*[pltpu.with_memory_space_constraint(a, pltpu.HBM) for a in operands])
    return out.reshape(query_rows.shape)


def solution(mesh):
    rows = P(None, ("grp", "seq"), None)
    return jax.shard_map(
        local,
        mesh=mesh,
        in_specs=(rows, rows, rows, rows, P(), P(), P(None, None, ("grp", "seq"))),
        out_specs=rows,
        check_vma=False,
    )
```

```python
import jax
import jax.numpy as jnp
from jax import lax
from jax.experimental import pallas as pl
from jax.experimental.pallas import tpu as pltpu
from jax.sharding import PartitionSpec as P

MESH = pl.DeviceIdType.MESH
F32 = jnp.float32
BF16 = jnp.bfloat16

NX, NZ, NG = 4, 8, 8
HEADS = 8
T = 128
SLICE = HEADS * T // (NX * NZ)
PER_HEAD = T // SLICE
PER_X = HEADS // NX
AUX = 2 * HEADS
HALF = NZ // 2
SIDE = HALF * SLICE
QUARTER = 2 * SIDE + AUX
OUTWARD = (
    (4, 2, 6, 3, 5, 1, 7, 0),
    (4, 6, 0, 2, 5, 3, 7, 1),
    (6, 0, 4, 5, 7, 1, 3, 2),
    (0, 6, 2, 4, 7, 1, 5, 3),
    (0, 2, 6, 1, 7, 3, 5, 4),
    (0, 2, 4, 6, 1, 3, 7, 5),
    (2, 0, 4, 1, 3, 5, 7, 6),
    (2, 4, 0, 6, 3, 1, 5, 7),
)
INWARD = (
    (0, 2, 6, 4, 1, 7, 3, 5),
    (0, 2, 4, 6, 1, 3, 7, 5),
    (2, 0, 4, 6, 1, 3, 5, 7),
    (2, 4, 0, 6, 3, 1, 5, 7),
    (4, 2, 6, 0, 3, 5, 1, 7),
    (4, 6, 0, 2, 5, 3, 7, 1),
    (6, 0, 4, 2, 5, 7, 1, 3),
    (0, 6, 2, 4, 7, 1, 5, 3),
)


def dot(a, b, dims=((1,), (0,))):
    return lax.dot_general(a, b, (dims, ((), ())), preferred_element_type=F32)


def lanes(h):
    return pl.ds(h * T, T)


def slice_row(c):
    return c * SLICE + (c // HALF) * AUX


def kernel(
    q_hbm, k_hbm, v_hbm, t_hbm, wq_hbm, wk_hbm, rate_hbm, o_ref,
    q_ref, k_ref, v_ref, t_ref, wq_ref, wk_ref, rate_ref,
    own, xin, tout, zin, gin, auxz, auxg, wout, cin, vout, fin,
    phiq, phik, run, run_col, den,
    s_in, s_az, r_az, s_ag, r_ag, s_x, r_x, s_z, r_z, s_g, r_g, s_w, r_w, s_v, r_v,
):
    g = lax.axis_index("grp")
    s = lax.axis_index("seq")
    z, x = s // NX, s % NX

    def at_x(i):
        return (g, z * NX + i)

    def at_z(i):
        return (g, i * NX + x)

    def at_g(i):
        return (i, s)

    def copy(src, dst, ssem, rsem, to):
        return pltpu.make_async_remote_copy(
            src_ref=src, dst_ref=dst, send_sem=ssem, recv_sem=rsem, device_id=to, device_id_type=MESH
        )

    other_x = [(x + d) % NX for d in (2, 1, 3)]
    low_x = [jnp.where(x <= n, n + 1, n) for n in range(NX - 1)]
    other_z = [(z + d) % NZ for d in (4, 3, 5, 2, 6, 1, 7)]
    other_g = [(g + d) % NG for d in (4, 3, 5, 2, 6, 1, 7)]

    barrier = pltpu.get_barrier_semaphore()
    for to in [at_x(i) for i in other_x] + [at_z(i) for i in other_z] + [at_g(i) for i in other_g]:
        pl.semaphore_signal(barrier, inc=1, device_id=to, device_id_type=MESH)

    pairs = [
        (rate_hbm, rate_ref), (wk_hbm, wk_ref), (k_hbm, k_ref), (v_hbm, v_ref),
        (wq_hbm, wq_ref), (q_hbm, q_ref), (t_hbm, t_ref),
    ]
    loads = [pltpu.make_async_copy(a, b, s_in.at[n]) for n, (a, b) in enumerate(pairs)]
    for load in loads:
        load.start()

    loads[0].wait()
    lane = lax.broadcasted_iota(jnp.int32, (HEADS, T), 1)
    running = rate_ref[...]
    step = 1
    while step < T:
        running = running + jnp.where(lane >= step, pltpu.roll(running, step, 1), 0.0)
        step *= 2
    total = jnp.broadcast_to(running[:, T - 1 : T], (HEADS, T))
    run[pl.ds(0, HEADS), :] = running
    fades = jnp.exp(running - total)

    loads[1].wait()
    loads[2].wait()
    loads[3].wait()
    sums = []
    for h in range(HEADS):
        product = dot(wk_ref[h], k_ref[:, lanes(h)], ((1,), (1,)))
        both = jnp.log1p(jnp.exp(-jnp.abs(product)))
        phi = jnp.concatenate([jnp.maximum(product, 0.0) + both, jnp.maximum(-product, 0.0) + both], axis=0)
        phi = phi.astype(BF16)
        phik[h] = phi
        fade = fades[h : h + 1, :]
        faded = phi.astype(F32) * fade
        at = slice_row((h % PER_X) * PER_HEAD)
        own[h // PER_X, pl.ds(at, T), :] = dot(faded.astype(BF16), v_ref[:, lanes(h)])
        high = fade.astype(BF16)
        low = (fade - high.astype(F32)).astype(BF16)
        pair = dot(jnp.concatenate([high, low], axis=0), phi, ((1,), (1,)))
        sums.append(pair[0:1, :] + pair[1:2, :])
    aux = jnp.concatenate(sums + [jnp.exp(-total)], axis=0)
    for p in range(NX):
        own[p, pl.ds(SIDE, AUX), :] = aux

    pl.semaphore_wait(barrier, len(other_x) + len(other_z) + len(other_g))

    def slots(table):
        def one(column):
            c = column[0]
            for i in range(1, NZ):
                c = jnp.where(z == i, column[i], c)
            return c

        return [one([row[n] for row in table]) for n in range(NZ)]

    order = slots(OUTWARD)

    def aux_to(i):
        at = pl.ds(SIDE, AUX)
        return copy(own.at[i, at], xin.at[x, at], s_x.at[0], r_x.at[NZ], at_x(i))

    def slice_at(c):
        return pl.ds(pl.multiple_of(slice_row(c), AUX), SLICE)

    def slice_to(i, c):
        at = slice_at(c)
        return copy(own.at[i, at], xin.at[x, at], s_x.at[0], r_x.at[c], at_x(i))

    for i in other_x:
        aux_to(i).start()
    for c in order:
        for i in other_x:
            slice_to(i, c).start()
    xin[x] = own[x]

    causal = lax.broadcasted_iota(jnp.int32, (T, T), 0) >= lax.broadcasted_iota(jnp.int32, (T, T), 1)

    def attend(start, end):
        for h in range(start, end):
            w = wq_ref[h]
            product = dot(q_ref[:, lanes(h)], jnp.concatenate([w, -w], axis=0), ((1,), (1,)))
            phi = (jnp.maximum(product, 0.0) + jnp.log1p(jnp.exp(-jnp.abs(product)))).astype(BF16)
            phiq[h] = phi
            row = run[pl.ds(h, 1), :]
            column = jnp.broadcast_to(row, (T, T)).T
            run_col[h] = column
            scores = dot(phi, phik[h])
            weighted = jnp.where(causal, scores * jnp.exp(row - column), 0.0)
            den[h] = jnp.broadcast_to(jnp.sum(weighted, axis=1, keepdims=True), (T, T))
            o_ref[:, lanes(h)] = dot(weighted.astype(BF16), v_ref[:, lanes(h)])

    loads[4].wait()
    loads[5].wait()
    loads[6].wait()
    attend(0, 4)

    def chain(ref, n, here, base):
        norm, decay = jnp.zeros((HEADS, T), F32), jnp.ones((HEADS, T), F32)
        norm_before, decay_before = norm, decay
        for i in range(n):
            norm_before = jnp.where(here == i, norm, norm_before)
            decay_before = jnp.where(here == i, decay, decay_before)
            d = ref[i, pl.ds(base + HEADS, HEADS), :]
            norm = d * norm + ref[i, pl.ds(base, HEADS), :]
            decay = d * decay
        return norm, decay, norm_before, decay_before

    def head_row(ref, i, base, c):
        return ref[i, pl.ds(base + HEADS + (x * NZ + c) // PER_HEAD, 1), :]

    def total_to_row(c):
        return copy(tout.at[c], zin.at[z], s_z.at[0], r_z.at[0], at_z(c))

    three = pl.ds(0, NX - 1)
    at = pl.ds(SIDE, AUX)
    copy(own.at[three, at], xin.at[three, at], s_x.at[0], r_x.at[NZ], at_x(other_x[0])).wait_recv()
    norm, decay, norm_x, decay_x = chain(xin, NX, x, SIDE)
    auxz[z, pl.ds(0, HEADS), :] = norm
    auxz[z, pl.ds(HEADS, HEADS), :] = decay
    for i in other_z:
        copy(auxz.at[z], auxz.at[z], s_az.at[0], r_az.at[0], at_z(i)).start()
    for c in order:
        at = slice_at(c)
        copy(own.at[three, at], xin.at[three, at], s_x.at[0], r_x.at[c], at_x(other_x[0])).wait_recv()
        acc = xin[0, at]
        for i in range(1, NX):
            acc = head_row(xin, i, SIDE, c) * acc + xin[i, at]
        tout[c] = acc

        @pl.when(c != z)
        def _(c=c):
            total_to_row(c).start()

    zin[z] = tout[z]

    def each_later(act):
        for d in (4, 5, 3, 2, 6, 1, 7):
            @pl.when(g + d < NG)
            def _(d=d):
                act(g + d)

    def each_earlier(act):
        for i in range(NG - 1):
            @pl.when(i < g)
            def _(i=i):
                act(i)

    def sums_to(i):
        return copy(auxg.at[g], auxg.at[g], s_ag.at[i], r_ag.at[g], at_g(i))

    def total_to(i):
        return copy(gin.at[g], gin.at[g], s_g.at[i], r_g.at[g], at_g(i))

    seven = pl.ds(0, NZ - 1)
    copy(auxz.at[seven], auxz.at[seven], s_az.at[0], r_az.at[0], at_z(other_z[0])).wait_recv()
    norm, decay, norm_z, decay_z = chain(auxz, NZ, z, 0)
    auxg[g, pl.ds(0, HEADS), :] = norm
    auxg[g, pl.ds(HEADS, HEADS), :] = decay
    each_later(lambda i: sums_to(i).start())
    copy(tout.at[seven], zin.at[seven], s_z.at[0], r_z.at[0], at_z(other_z[0])).wait_recv()
    acc = zin[0]
    for i in range(1, NZ):
        acc = head_row(auxz, i, 0, z) * acc + zin[i]
    gin[g] = acc
    each_later(lambda i: total_to(i).start())
    attend(4, HEADS)

    each_earlier(lambda i: copy(auxg.at[g], auxg.at[i], s_ag.at[i], r_ag.at[i], at_g(i)).wait_recv())
    each_earlier(lambda i: copy(gin.at[g], gin.at[i], s_g.at[i], r_g.at[i], at_g(i)).wait_recv())
    acc = jnp.zeros((SLICE, T), F32)
    for i in range(NG - 1):
        acc = jnp.where(i < g, head_row(auxg, i, 0, z) * acc + gin[i], acc)

    def carry_to(i):
        return copy(wout.at[i], cin.at[z], s_w.at[0], r_w.at[z], at_z(i))

    wout[0] = acc

    @pl.when(z != 0)
    def _():
        carry_to(0).start()

    for i in range(1, NZ):
        acc = head_row(auxz, i - 1, 0, z) * acc + zin[i - 1]
        wout[i] = acc
    for i in range(1, NZ):
        @pl.when(i != z)
        def _(i=i):
            carry_to(i).start()

    cin[z] = wout[z]

    inward = slots(INWARD)

    def forward(c):
        @pl.when(c != z)
        def _(c=c):
            copy(wout.at[0], cin.at[c], s_w.at[0], r_w.at[c], at_z(c)).wait_recv()

        at = slice_at(c)
        acc = cin[c]
        for i in range(NX):
            vout[i, c] = acc
            if i < NX - 1:
                acc = head_row(xin, i, SIDE, c) * acc + xin[i, at]
        for i in low_x:
            copy(vout.at[i, c], fin.at[x, c], s_v.at[0], r_v.at[x], at_x(i)).start()

    for c in inward[:HALF]:
        forward(c)

    norm_g = jnp.zeros((HEADS, T), F32)
    for i in range(NG - 1):
        arrived = auxg[i, pl.ds(HEADS, HEADS), :] * norm_g + auxg[i, pl.ds(0, HEADS), :]
        norm_g = jnp.where(i < g, arrived, norm_g)
    norm_in = decay_x * (decay_z * norm_g + norm_z) + norm_x
    for h in range(HEADS):
        lead = jnp.exp(-run_col[h])
        from_norm = jnp.sum(phiq[h].astype(F32) * norm_in[h : h + 1, :], axis=1, keepdims=True)
        inverse = 1.0 / (den[h] + lead * from_norm)
        o_ref[:, lanes(h)] = o_ref[:, lanes(h)] * inverse - t_ref[:, lanes(h)].astype(F32)
        den[h] = lead * inverse

    for c in inward[HALF:]:
        forward(c)

    def finish(p, states):
        for e in range(PER_X):
            h = PER_X * p + e
            state = states[pl.ds(e * PER_HEAD, PER_HEAD)].reshape(T, T)
            high = state.astype(BF16)
            low = (state - high.astype(F32)).astype(BF16)
            phi = phiq[h]
            at = pl.ds(pl.multiple_of(h * T, T), T)
            product = dot(jnp.concatenate([phi, phi], axis=1), jnp.concatenate([high, low], axis=0))
            o_ref[:, at] = o_ref[:, at] + den[h] * product

    finish(x, vout.at[x])
    for p in (other_x[1], other_x[2], other_x[0]):
        copy(vout.at[0], fin.at[p], s_v.at[0], r_v.at[p], at_x(p)).wait_recv()
        finish(p, fin.at[p])

    to = at_x(other_x[0])
    copy(own.at[three], xin.at[three], s_x.at[0], r_x.at[0], to).wait_send()
    copy(vout.at[three], fin.at[three], s_v.at[0], r_v.at[0], to).wait_send()
    copy(tout.at[seven], zin.at[seven], s_z.at[0], r_z.at[0], at_z(other_z[0])).wait_send()
    copy(wout.at[seven], cin.at[seven], s_w.at[0], r_w.at[0], at_z(other_z[0])).wait_send()
    each_later(lambda i: total_to(i).wait_send())
    each_later(lambda i: sums_to(i).wait_send())
    copy(auxz.at[seven], auxz.at[seven], s_az.at[0], r_az.at[0], at_z(other_z[0])).wait_send()


def local(query_rows, key_rows, value_rows, teacher, query_map, key_map, decay_rate):
    rows = query_rows.shape[1:]
    operands = (
        query_rows.reshape(rows),
        key_rows.reshape(rows),
        value_rows.reshape(rows),
        teacher.reshape(rows),
        jnp.swapaxes(query_map, 1, 2),
        jnp.swapaxes(key_map, 1, 2),
        decay_rate.reshape(decay_rate.shape[1:]),
    )
    dma = lambda n: pltpu.SemaphoreType.DMA((n,))
    part = lambda *lead: pltpu.VMEM(lead + (SLICE, T), F32)
    rowed = lambda *lead: pltpu.VMEM(lead + (T,), F32)
    out = pl.pallas_call(
        kernel,
        out_shape=jax.ShapeDtypeStruct(rows, F32),
        in_specs=[pl.BlockSpec(memory_space=pltpu.HBM)] * 7,
        out_specs=pl.BlockSpec(memory_space=pltpu.VMEM),
        scratch_shapes=[pltpu.VMEM(a.shape, a.dtype) for a in operands]
        + [
            rowed(NX, QUARTER), rowed(NX, QUARTER),
            part(NZ), part(NZ), part(NG), rowed(NZ, AUX), rowed(NG, AUX),
            part(NZ), part(NZ), part(NX, NZ), part(NX, NZ),
            pltpu.VMEM((HEADS, T, T), BF16), pltpu.VMEM((HEADS, T, T), BF16),
            rowed(HEADS), rowed(HEADS, T), rowed(HEADS, T),
            dma(7), dma(1), dma(1), dma(NG), dma(NG), dma(1), dma(NZ + 1), dma(1), dma(1), dma(NG), dma(NG),
            dma(1), dma(NZ), dma(1), dma(NX),
        ],
        compiler_params=pltpu.CompilerParams(
            collective_id=0, has_side_effects=True, vmem_limit_bytes=32 * 1024 * 1024
        ),
    )(*[pltpu.with_memory_space_constraint(a, pltpu.HBM) for a in operands])
    return out.reshape(query_rows.shape)


def solution(mesh):
    rows = P(None, ("grp", "seq"), None)
    return jax.shard_map(
        local,
        mesh=mesh,
        in_specs=(rows, rows, rows, rows, P(), P(), P(None, None, ("grp", "seq"))),
        out_specs=rows,
        check_vma=False,
    )
```

```python
import jax
import jax.numpy as jnp
from jax import lax
from jax.experimental import pallas as pl
from jax.experimental.pallas import tpu as pltpu
from jax.sharding import PartitionSpec as P

MESH = pl.DeviceIdType.MESH
F32 = jnp.float32
BF16 = jnp.bfloat16

NX, NZ, NG = 4, 8, 8
HEADS = 8
T = 128
SLICE = HEADS * T // (NX * NZ)
PER_HEAD = T // SLICE
PER_X = HEADS // NX
AUX = 2 * HEADS
HALF = NZ // 2
SIDE = HALF * SLICE
QUARTER = 2 * SIDE + AUX
OUTWARD = (
    (4, 2, 6, 3, 5, 1, 7, 0),
    (4, 6, 0, 2, 5, 3, 7, 1),
    (6, 0, 4, 5, 7, 1, 3, 2),
    (0, 6, 2, 4, 7, 1, 5, 3),
    (0, 2, 6, 1, 7, 3, 5, 4),
    (0, 2, 4, 6, 1, 3, 7, 5),
    (2, 0, 4, 1, 3, 5, 7, 6),
    (2, 4, 0, 6, 3, 1, 5, 7),
)
INWARD = (
    (0, 2, 6, 4, 1, 7, 3, 5),
    (0, 2, 4, 6, 1, 3, 7, 5),
    (2, 0, 4, 6, 1, 3, 5, 7),
    (2, 4, 0, 6, 3, 1, 5, 7),
    (4, 2, 6, 0, 3, 5, 1, 7),
    (4, 6, 0, 2, 5, 3, 7, 1),
    (6, 0, 4, 2, 5, 7, 1, 3),
    (0, 6, 2, 4, 7, 1, 5, 3),
)


def dot(a, b, dims=((1,), (0,))):
    return lax.dot_general(a, b, (dims, ((), ())), preferred_element_type=F32)


def lanes(h):
    return pl.ds(h * T, T)


def slice_row(c):
    return c * SLICE + (c // HALF) * AUX


def kernel(
    q_hbm, k_hbm, v_hbm, t_hbm, wq_hbm, wk_hbm, rate_hbm, o_ref,
    q_ref, k_ref, v_ref, t_ref, wq_ref, wk_ref, rate_ref,
    own, xin, tout, zin, gin, auxz, auxg, wout, cin, vout, fin,
    phiq, phik, run, run_col, den,
    s_in, s_az, r_az, s_ag, r_ag, s_x, r_x, s_z, r_z, s_g, r_g, s_w, r_w, s_v, r_v,
):
    g = lax.axis_index("grp")
    s = lax.axis_index("seq")
    z, x = s // NX, s % NX

    def at_x(i):
        return (g, z * NX + i)

    def at_z(i):
        return (g, i * NX + x)

    def at_g(i):
        return (i, s)

    def copy(src, dst, ssem, rsem, to):
        return pltpu.make_async_remote_copy(
            src_ref=src, dst_ref=dst, send_sem=ssem, recv_sem=rsem, device_id=to, device_id_type=MESH
        )

    other_x = [(x + d) % NX for d in (2, 1, 3)]
    low_x = [jnp.where(x <= n, n + 1, n) for n in range(NX - 1)]
    other_z = [(z + d) % NZ for d in (4, 3, 5, 2, 6, 1, 7)]
    other_g = [(g + d) % NG for d in (4, 3, 5, 2, 6, 1, 7)]

    barrier = pltpu.get_barrier_semaphore()
    for to in [at_x(i) for i in other_x] + [at_z(i) for i in other_z] + [at_g(i) for i in other_g]:
        pl.semaphore_signal(barrier, inc=1, device_id=to, device_id_type=MESH)

    pairs = [
        (rate_hbm, rate_ref), (wk_hbm, wk_ref), (k_hbm, k_ref), (v_hbm, v_ref),
        (wq_hbm, wq_ref), (q_hbm, q_ref), (t_hbm, t_ref),
    ]
    loads = [pltpu.make_async_copy(a, b, s_in.at[n]) for n, (a, b) in enumerate(pairs)]
    for load in loads:
        load.start()

    loads[0].wait()
    lane = lax.broadcasted_iota(jnp.int32, (HEADS, T), 1)
    running = rate_ref[...]
    step = 1
    while step < T:
        running = running + jnp.where(lane >= step, pltpu.roll(running, step, 1), 0.0)
        step *= 2
    total = jnp.broadcast_to(running[:, T - 1 : T], (HEADS, T))
    run[pl.ds(0, HEADS), :] = running
    fades = jnp.exp(running - total)

    loads[1].wait()
    loads[2].wait()
    loads[3].wait()
    sums = []
    for h in range(HEADS):
        product = dot(wk_ref[h], k_ref[:, lanes(h)], ((1,), (1,)))
        both = jnp.log1p(jnp.exp(-jnp.abs(product)))
        phi = jnp.concatenate([jnp.maximum(product, 0.0) + both, jnp.maximum(-product, 0.0) + both], axis=0)
        phi = phi.astype(BF16)
        phik[h] = phi
        fade = fades[h : h + 1, :]
        faded = phi.astype(F32) * fade
        at = slice_row((h % PER_X) * PER_HEAD)
        own[h // PER_X, pl.ds(at, T), :] = dot(faded.astype(BF16), v_ref[:, lanes(h)])
        high = fade.astype(BF16)
        low = (fade - high.astype(F32)).astype(BF16)
        pair = dot(jnp.concatenate([high, low], axis=0), phi, ((1,), (1,)))
        sums.append(pair[0:1, :] + pair[1:2, :])
    aux = jnp.concatenate(sums + [jnp.exp(-total)], axis=0)
    for p in range(NX):
        own[p, pl.ds(SIDE, AUX), :] = aux

    pl.semaphore_wait(barrier, len(other_x) + len(other_z) + len(other_g))

    def slots(table):
        def one(column):
            c = column[0]
            for i in range(1, NZ):
                c = jnp.where(z == i, column[i], c)
            return c

        return [one([row[n] for row in table]) for n in range(NZ)]

    order = slots(OUTWARD)

    def aux_to(i):
        at = pl.ds(SIDE, AUX)
        return copy(own.at[i, at], xin.at[x, at], s_x.at[0], r_x.at[NZ], at_x(i))

    def slice_at(c):
        return pl.ds(pl.multiple_of(slice_row(c), AUX), SLICE)

    def slice_to(i, c):
        at = slice_at(c)
        return copy(own.at[i, at], xin.at[x, at], s_x.at[0], r_x.at[c], at_x(i))

    for i in other_x:
        aux_to(i).start()
    for c in order:
        for i in other_x:
            slice_to(i, c).start()
    xin[x] = own[x]

    causal = lax.broadcasted_iota(jnp.int32, (T, T), 0) >= lax.broadcasted_iota(jnp.int32, (T, T), 1)

    def attend(start, end):
        for h in range(start, end):
            w = wq_ref[h]
            product = dot(q_ref[:, lanes(h)], jnp.concatenate([w, -w], axis=0), ((1,), (1,)))
            phi = (jnp.maximum(product, 0.0) + jnp.log1p(jnp.exp(-jnp.abs(product)))).astype(BF16)
            phiq[h] = phi
            row = run[pl.ds(h, 1), :]
            column = jnp.broadcast_to(row, (T, T)).T
            run_col[h] = column
            scores = dot(phi, phik[h])
            weighted = jnp.where(causal, scores * jnp.exp(row - column), 0.0)
            den[h] = jnp.broadcast_to(jnp.sum(weighted, axis=1, keepdims=True), (T, T))
            o_ref[:, lanes(h)] = dot(weighted.astype(BF16), v_ref[:, lanes(h)])

    loads[4].wait()
    loads[5].wait()
    loads[6].wait()
    attend(0, 4)

    def chain(ref, n, here, base):
        norm, decay = jnp.zeros((HEADS, T), F32), jnp.ones((HEADS, T), F32)
        norm_before, decay_before = norm, decay
        for i in range(n):
            norm_before = jnp.where(here == i, norm, norm_before)
            decay_before = jnp.where(here == i, decay, decay_before)
            d = ref[i, pl.ds(base + HEADS, HEADS), :]
            norm = d * norm + ref[i, pl.ds(base, HEADS), :]
            decay = d * decay
        return norm, decay, norm_before, decay_before

    def head_row(ref, i, base, c):
        return ref[i, pl.ds(base + HEADS + (x * NZ + c) // PER_HEAD, 1), :]

    def total_to_row(c):
        return copy(tout.at[c], zin.at[z], s_z.at[0], r_z.at[0], at_z(c))

    three = pl.ds(0, NX - 1)
    at = pl.ds(SIDE, AUX)
    copy(own.at[three, at], xin.at[three, at], s_x.at[0], r_x.at[NZ], at_x(other_x[0])).wait_recv()
    norm, decay, norm_x, decay_x = chain(xin, NX, x, SIDE)
    auxz[z, pl.ds(0, HEADS), :] = norm
    auxz[z, pl.ds(HEADS, HEADS), :] = decay
    for i in other_z:
        copy(auxz.at[z], auxz.at[z], s_az.at[0], r_az.at[0], at_z(i)).start()
    for c in order:
        at = slice_at(c)
        copy(own.at[three, at], xin.at[three, at], s_x.at[0], r_x.at[c], at_x(other_x[0])).wait_recv()
        acc = xin[0, at]
        for i in range(1, NX):
            acc = head_row(xin, i, SIDE, c) * acc + xin[i, at]
        tout[c] = acc

        @pl.when(c != z)
        def _(c=c):
            total_to_row(c).start()

    zin[z] = tout[z]

    def each_later(act):
        for d in (4, 5, 3, 2, 6, 1, 7):
            @pl.when(g + d < NG)
            def _(d=d):
                act(g + d)

    def from_earlier(act):
        for n in range(1, NG):
            @pl.when(g == n)
            def _(n=n):
                act(n)

    def to_later(act):
        for n in range(1, NG):
            @pl.when(g == NG - 1 - n)
            def _(n=n):
                act(n)

    def sums_of(n):
        some = pl.ds(0, n)
        return copy(auxg.at[some], auxg.at[some], s_ag.at[0], r_ag.at[0], at_g(other_g[0]))

    def totals_of(n):
        some = pl.ds(0, n)
        return copy(gin.at[some], gin.at[some], s_g.at[0], r_g.at[0], at_g(other_g[0]))

    def sums_to(i):
        return copy(auxg.at[g], auxg.at[g], s_ag.at[0], r_ag.at[0], at_g(i))

    def total_to(i):
        return copy(gin.at[g], gin.at[g], s_g.at[0], r_g.at[0], at_g(i))

    seven = pl.ds(0, NZ - 1)
    copy(auxz.at[seven], auxz.at[seven], s_az.at[0], r_az.at[0], at_z(other_z[0])).wait_recv()
    norm, decay, norm_z, decay_z = chain(auxz, NZ, z, 0)
    auxg[g, pl.ds(0, HEADS), :] = norm
    auxg[g, pl.ds(HEADS, HEADS), :] = decay
    each_later(lambda i: sums_to(i).start())
    copy(tout.at[seven], zin.at[seven], s_z.at[0], r_z.at[0], at_z(other_z[0])).wait_recv()
    acc = zin[0]
    for i in range(1, NZ):
        acc = head_row(auxz, i, 0, z) * acc + zin[i]
    gin[g] = acc
    each_later(lambda i: total_to(i).start())
    attend(4, HEADS)

    from_earlier(lambda n: sums_of(n).wait_recv())
    from_earlier(lambda n: totals_of(n).wait_recv())
    acc = jnp.zeros((SLICE, T), F32)
    for i in range(NG - 1):
        acc = jnp.where(i < g, head_row(auxg, i, 0, z) * acc + gin[i], acc)

    def carry_to(i):
        return copy(wout.at[i], cin.at[z], s_w.at[0], r_w.at[z], at_z(i))

    wout[0] = acc

    @pl.when(z != 0)
    def _():
        carry_to(0).start()

    for i in range(1, NZ):
        acc = head_row(auxz, i - 1, 0, z) * acc + zin[i - 1]
        wout[i] = acc
    for i in range(1, NZ):
        @pl.when(i != z)
        def _(i=i):
            carry_to(i).start()

    cin[z] = wout[z]

    inward = slots(INWARD)

    def forward(c):
        @pl.when(c != z)
        def _(c=c):
            copy(wout.at[0], cin.at[c], s_w.at[0], r_w.at[c], at_z(c)).wait_recv()

        at = slice_at(c)
        acc = cin[c]
        for i in range(NX):
            vout[i, c] = acc
            if i < NX - 1:
                acc = head_row(xin, i, SIDE, c) * acc + xin[i, at]
        for i in low_x:
            copy(vout.at[i, c], fin.at[x, c], s_v.at[0], r_v.at[x], at_x(i)).start()

    for c in inward[:HALF]:
        forward(c)

    norm_g = jnp.zeros((HEADS, T), F32)
    for i in range(NG - 1):
        arrived = auxg[i, pl.ds(HEADS, HEADS), :] * norm_g + auxg[i, pl.ds(0, HEADS), :]
        norm_g = jnp.where(i < g, arrived, norm_g)
    norm_in = decay_x * (decay_z * norm_g + norm_z) + norm_x
    for h in range(HEADS):
        lead = jnp.exp(-run_col[h])
        from_norm = jnp.sum(phiq[h].astype(F32) * norm_in[h : h + 1, :], axis=1, keepdims=True)
        inverse = 1.0 / (den[h] + lead * from_norm)
        o_ref[:, lanes(h)] = o_ref[:, lanes(h)] * inverse - t_ref[:, lanes(h)].astype(F32)
        den[h] = lead * inverse

    for c in inward[HALF:]:
        forward(c)

    def finish(p, states):
        for e in range(PER_X):
            h = PER_X * p + e
            state = states[pl.ds(e * PER_HEAD, PER_HEAD)].reshape(T, T)
            high = state.astype(BF16)
            low = (state - high.astype(F32)).astype(BF16)
            phi = phiq[h]
            at = pl.ds(pl.multiple_of(h * T, T), T)
            product = dot(jnp.concatenate([phi, phi], axis=1), jnp.concatenate([high, low], axis=0))
            o_ref[:, at] = o_ref[:, at] + den[h] * product

    finish(x, vout.at[x])
    for p in (other_x[1], other_x[2], other_x[0]):
        copy(vout.at[0], fin.at[p], s_v.at[0], r_v.at[p], at_x(p)).wait_recv()
        finish(p, fin.at[p])

    to = at_x(other_x[0])
    copy(own.at[three], xin.at[three], s_x.at[0], r_x.at[0], to).wait_send()
    copy(vout.at[three], fin.at[three], s_v.at[0], r_v.at[0], to).wait_send()
    copy(tout.at[seven], zin.at[seven], s_z.at[0], r_z.at[0], at_z(other_z[0])).wait_send()
    copy(wout.at[seven], cin.at[seven], s_w.at[0], r_w.at[0], at_z(other_z[0])).wait_send()
    to_later(lambda n: totals_of(n).wait_send())
    to_later(lambda n: sums_of(n).wait_send())
    copy(auxz.at[seven], auxz.at[seven], s_az.at[0], r_az.at[0], at_z(other_z[0])).wait_send()


def local(query_rows, key_rows, value_rows, teacher, query_map, key_map, decay_rate):
    rows = query_rows.shape[1:]
    operands = (
        query_rows.reshape(rows),
        key_rows.reshape(rows),
        value_rows.reshape(rows),
        teacher.reshape(rows),
        jnp.swapaxes(query_map, 1, 2),
        jnp.swapaxes(key_map, 1, 2),
        decay_rate.reshape(decay_rate.shape[1:]),
    )
    dma = lambda n: pltpu.SemaphoreType.DMA((n,))
    part = lambda *lead: pltpu.VMEM(lead + (SLICE, T), F32)
    rowed = lambda *lead: pltpu.VMEM(lead + (T,), F32)
    out = pl.pallas_call(
        kernel,
        out_shape=jax.ShapeDtypeStruct(rows, F32),
        in_specs=[pl.BlockSpec(memory_space=pltpu.HBM)] * 7,
        out_specs=pl.BlockSpec(memory_space=pltpu.VMEM),
        scratch_shapes=[pltpu.VMEM(a.shape, a.dtype) for a in operands]
        + [
            rowed(NX, QUARTER), rowed(NX, QUARTER),
            part(NZ), part(NZ), part(NG), rowed(NZ, AUX), rowed(NG, AUX),
            part(NZ), part(NZ), part(NX, NZ), part(NX, NZ),
            pltpu.VMEM((HEADS, T, T), BF16), pltpu.VMEM((HEADS, T, T), BF16),
            rowed(HEADS), rowed(HEADS, T), rowed(HEADS, T),
            dma(7), dma(1), dma(1), dma(1), dma(1), dma(1), dma(NZ + 1), dma(1), dma(1), dma(1), dma(1),
            dma(1), dma(NZ), dma(1), dma(NX),
        ],
        compiler_params=pltpu.CompilerParams(
            collective_id=0, has_side_effects=True, vmem_limit_bytes=32 * 1024 * 1024
        ),
    )(*[pltpu.with_memory_space_constraint(a, pltpu.HBM) for a in operands])
    return out.reshape(query_rows.shape)


def solution(mesh):
    rows = P(None, ("grp", "seq"), None)
    return jax.shard_map(
        local,
        mesh=mesh,
        in_specs=(rows, rows, rows, rows, P(), P(), P(None, None, ("grp", "seq"))),
        out_specs=rows,
        check_vma=False,
    )
```

```python
import jax
import jax.numpy as jnp
from jax import lax
from jax.experimental import pallas as pl
from jax.experimental.pallas import tpu as pltpu
from jax.sharding import PartitionSpec as P

MESH = pl.DeviceIdType.MESH
F32 = jnp.float32
BF16 = jnp.bfloat16

NX, NZ, NG = 4, 8, 8
HEADS = 8
T = 128
SLICE = HEADS * T // (NX * NZ)
PER_HEAD = T // SLICE
PER_X = HEADS // NX
AUX = 2 * HEADS
HALF = NZ // 2
SIDE = HALF * SLICE
QUARTER = 2 * SIDE + AUX
OUTWARD = (
    (4, 2, 6, 3, 5, 1, 7, 0),
    (4, 6, 0, 2, 5, 3, 7, 1),
    (6, 0, 4, 5, 7, 1, 3, 2),
    (0, 6, 2, 4, 7, 1, 5, 3),
    (0, 2, 6, 1, 7, 3, 5, 4),
    (0, 2, 4, 6, 1, 3, 7, 5),
    (2, 0, 4, 1, 3, 5, 7, 6),
    (2, 4, 0, 6, 3, 1, 5, 7),
)
INWARD = (
    (0, 2, 6, 4, 1, 7, 3, 5),
    (0, 2, 4, 6, 1, 3, 7, 5),
    (2, 0, 4, 6, 1, 3, 5, 7),
    (2, 4, 0, 6, 3, 1, 5, 7),
    (4, 2, 6, 0, 3, 5, 1, 7),
    (4, 6, 0, 2, 5, 3, 7, 1),
    (6, 0, 4, 2, 5, 7, 1, 3),
    (0, 6, 2, 4, 7, 1, 5, 3),
)


def dot(a, b, dims=((1,), (0,))):
    return lax.dot_general(a, b, (dims, ((), ())), preferred_element_type=F32)


def lanes(h):
    return pl.ds(h * T, T)


def slice_row(c):
    return c * SLICE + (c // HALF) * AUX


def kernel(
    q_hbm, k_hbm, v_hbm, t_hbm, wq_hbm, wk_hbm, rate_hbm, o_ref,
    q_ref, k_ref, v_ref, t_ref, wq_ref, wk_ref, rate_ref,
    own, xin, tout, zin, gin, auxz, auxg, wout, cin, vout, fin,
    phiq, phik, run, run_col, den,
    s_in, s_az, r_az, s_ag, r_ag, s_x, r_x, s_z, r_z, s_g, r_g, s_w, r_w, s_v, r_v,
):
    g = lax.axis_index("grp")
    s = lax.axis_index("seq")
    z, x = s // NX, s % NX

    def at_x(i):
        return (g, z * NX + i)

    def at_z(i):
        return (g, i * NX + x)

    def at_g(i):
        return (i, s)

    def copy(src, dst, ssem, rsem, to):
        return pltpu.make_async_remote_copy(
            src_ref=src, dst_ref=dst, send_sem=ssem, recv_sem=rsem, device_id=to, device_id_type=MESH
        )

    other_x = [(x + d) % NX for d in (2, 1, 3)]
    low_x = [jnp.where(x <= n, n + 1, n) for n in range(NX - 1)]
    other_z = [(z + d) % NZ for d in (4, 3, 5, 2, 6, 1, 7)]
    other_g = [(g + d) % NG for d in (4, 3, 5, 2, 6, 1, 7)]

    barrier = pltpu.get_barrier_semaphore()
    for to in [at_x(i) for i in other_x] + [at_z(i) for i in other_z]:
        pl.semaphore_signal(barrier, inc=1, device_id=to, device_id_type=MESH)
    for i in range(NG - 1):
        @pl.when(i < g)
        def _(i=i):
            pl.semaphore_signal(barrier, inc=1, device_id=at_g(i), device_id_type=MESH)

    pairs = [
        (rate_hbm, rate_ref), (wk_hbm, wk_ref), (k_hbm, k_ref), (v_hbm, v_ref),
        (wq_hbm, wq_ref), (q_hbm, q_ref), (t_hbm, t_ref),
    ]
    loads = [pltpu.make_async_copy(a, b, s_in.at[n]) for n, (a, b) in enumerate(pairs)]
    for load in loads:
        load.start()

    loads[0].wait()
    lane = lax.broadcasted_iota(jnp.int32, (HEADS, T), 1)
    running = rate_ref[...]
    step = 1
    while step < T:
        running = running + jnp.where(lane >= step, pltpu.roll(running, step, 1), 0.0)
        step *= 2
    total = jnp.broadcast_to(running[:, T - 1 : T], (HEADS, T))
    run[pl.ds(0, HEADS), :] = running
    fades = jnp.exp(running - total)

    loads[1].wait()
    loads[2].wait()
    loads[3].wait()
    sums = []
    for h in range(HEADS):
        product = dot(wk_ref[h], k_ref[:, lanes(h)], ((1,), (1,)))
        both = jnp.log1p(jnp.exp(-jnp.abs(product)))
        phi = jnp.concatenate([jnp.maximum(product, 0.0) + both, jnp.maximum(-product, 0.0) + both], axis=0)
        phi = phi.astype(BF16)
        phik[h] = phi
        fade = fades[h : h + 1, :]
        faded = phi.astype(F32) * fade
        at = slice_row((h % PER_X) * PER_HEAD)
        own[h // PER_X, pl.ds(at, T), :] = dot(faded.astype(BF16), v_ref[:, lanes(h)])
        high = fade.astype(BF16)
        low = (fade - high.astype(F32)).astype(BF16)
        pair = dot(jnp.concatenate([high, low], axis=0), phi, ((1,), (1,)))
        sums.append(pair[0:1, :] + pair[1:2, :])
    aux = jnp.concatenate(sums + [jnp.exp(-total)], axis=0)
    for p in range(NX):
        own[p, pl.ds(SIDE, AUX), :] = aux

    pl.semaphore_wait(barrier, NX - 1 + NZ - 1 + NG - 1 - g)

    def slots(table):
        def one(column):
            c = column[0]
            for i in range(1, NZ):
                c = jnp.where(z == i, column[i], c)
            return c

        return [one([row[n] for row in table]) for n in range(NZ)]

    order = slots(OUTWARD)

    def aux_to(i):
        at = pl.ds(SIDE, AUX)
        return copy(own.at[i, at], xin.at[x, at], s_x.at[0], r_x.at[NZ], at_x(i))

    def slice_at(c):
        return pl.ds(pl.multiple_of(slice_row(c), AUX), SLICE)

    def slice_to(i, c):
        at = slice_at(c)
        return copy(own.at[i, at], xin.at[x, at], s_x.at[0], r_x.at[c], at_x(i))

    for i in other_x:
        aux_to(i).start()
    for c in order:
        for i in other_x:
            slice_to(i, c).start()
    xin[x] = own[x]

    causal = lax.broadcasted_iota(jnp.int32, (T, T), 0) >= lax.broadcasted_iota(jnp.int32, (T, T), 1)

    def attend(start, end):
        for h in range(start, end):
            w = wq_ref[h]
            product = dot(q_ref[:, lanes(h)], jnp.concatenate([w, -w], axis=0), ((1,), (1,)))
            phi = (jnp.maximum(product, 0.0) + jnp.log1p(jnp.exp(-jnp.abs(product)))).astype(BF16)
            phiq[h] = phi
            row = run[pl.ds(h, 1), :]
            column = jnp.broadcast_to(row, (T, T)).T
            run_col[h] = column
            scores = dot(phi, phik[h])
            weighted = jnp.where(causal, scores * jnp.exp(row - column), 0.0)
            den[h] = jnp.broadcast_to(jnp.sum(weighted, axis=1, keepdims=True), (T, T))
            o_ref[:, lanes(h)] = dot(weighted.astype(BF16), v_ref[:, lanes(h)])

    loads[4].wait()
    loads[5].wait()
    loads[6].wait()
    attend(0, 4)

    def chain(ref, n, here, base):
        norm, decay = jnp.zeros((HEADS, T), F32), jnp.ones((HEADS, T), F32)
        norm_before, decay_before = norm, decay
        for i in range(n):
            norm_before = jnp.where(here == i, norm, norm_before)
            decay_before = jnp.where(here == i, decay, decay_before)
            d = ref[i, pl.ds(base + HEADS, HEADS), :]
            norm = d * norm + ref[i, pl.ds(base, HEADS), :]
            decay = d * decay
        return norm, decay, norm_before, decay_before

    def head_row(ref, i, base, c):
        return ref[i, pl.ds(base + HEADS + (x * NZ + c) // PER_HEAD, 1), :]

    def total_to_row(c):
        return copy(tout.at[c], zin.at[z], s_z.at[0], r_z.at[0], at_z(c))

    three = pl.ds(0, NX - 1)
    at = pl.ds(SIDE, AUX)
    copy(own.at[three, at], xin.at[three, at], s_x.at[0], r_x.at[NZ], at_x(other_x[0])).wait_recv()
    norm, decay, norm_x, decay_x = chain(xin, NX, x, SIDE)
    auxz[z, pl.ds(0, HEADS), :] = norm
    auxz[z, pl.ds(HEADS, HEADS), :] = decay
    for i in other_z:
        copy(auxz.at[z], auxz.at[z], s_az.at[0], r_az.at[0], at_z(i)).start()
    for c in order:
        at = slice_at(c)
        copy(own.at[three, at], xin.at[three, at], s_x.at[0], r_x.at[c], at_x(other_x[0])).wait_recv()
        acc = xin[0, at]
        for i in range(1, NX):
            acc = head_row(xin, i, SIDE, c) * acc + xin[i, at]
        tout[c] = acc

        @pl.when(c != z)
        def _(c=c):
            total_to_row(c).start()

    zin[z] = tout[z]

    def each_later(act):
        for d in (4, 5, 3, 2, 6, 1, 7):
            @pl.when(g + d < NG)
            def _(d=d):
                act(g + d)

    def from_earlier(act):
        for n in range(1, NG):
            @pl.when(g == n)
            def _(n=n):
                act(n)

    def to_later(act):
        for n in range(1, NG):
            @pl.when(g == NG - 1 - n)
            def _(n=n):
                act(n)

    def sums_of(n):
        some = pl.ds(0, n)
        return copy(auxg.at[some], auxg.at[some], s_ag.at[0], r_ag.at[0], at_g(other_g[0]))

    def totals_of(n):
        some = pl.ds(0, n)
        return copy(gin.at[some], gin.at[some], s_g.at[0], r_g.at[0], at_g(other_g[0]))

    def sums_to(i):
        return copy(auxg.at[g], auxg.at[g], s_ag.at[0], r_ag.at[0], at_g(i))

    def total_to(i):
        return copy(gin.at[g], gin.at[g], s_g.at[0], r_g.at[0], at_g(i))

    seven = pl.ds(0, NZ - 1)
    copy(auxz.at[seven], auxz.at[seven], s_az.at[0], r_az.at[0], at_z(other_z[0])).wait_recv()
    norm, decay, norm_z, decay_z = chain(auxz, NZ, z, 0)
    auxg[g, pl.ds(0, HEADS), :] = norm
    auxg[g, pl.ds(HEADS, HEADS), :] = decay
    each_later(lambda i: sums_to(i).start())
    copy(tout.at[seven], zin.at[seven], s_z.at[0], r_z.at[0], at_z(other_z[0])).wait_recv()
    acc = zin[0]
    for i in range(1, NZ):
        acc = head_row(auxz, i, 0, z) * acc + zin[i]
    gin[g] = acc
    each_later(lambda i: total_to(i).start())
    attend(4, HEADS)

    from_earlier(lambda n: sums_of(n).wait_recv())
    from_earlier(lambda n: totals_of(n).wait_recv())
    acc = jnp.zeros((SLICE, T), F32)
    for i in range(NG - 1):
        acc = jnp.where(i < g, head_row(auxg, i, 0, z) * acc + gin[i], acc)

    def carry_to(i):
        return copy(wout.at[i], cin.at[z], s_w.at[0], r_w.at[z], at_z(i))

    wout[0] = acc

    @pl.when(z != 0)
    def _():
        carry_to(0).start()

    for i in range(1, NZ):
        acc = head_row(auxz, i - 1, 0, z) * acc + zin[i - 1]
        wout[i] = acc
    for i in range(1, NZ):
        @pl.when(i != z)
        def _(i=i):
            carry_to(i).start()

    cin[z] = wout[z]

    inward = slots(INWARD)

    def forward(c):
        @pl.when(c != z)
        def _(c=c):
            copy(wout.at[0], cin.at[c], s_w.at[0], r_w.at[c], at_z(c)).wait_recv()

        at = slice_at(c)
        acc = cin[c]
        for i in range(NX):
            vout[i, c] = acc
            if i < NX - 1:
                acc = head_row(xin, i, SIDE, c) * acc + xin[i, at]
        for i in low_x:
            copy(vout.at[i, c], fin.at[x, c], s_v.at[0], r_v.at[x], at_x(i)).start()

    for c in inward[:HALF]:
        forward(c)

    norm_g = jnp.zeros((HEADS, T), F32)
    for i in range(NG - 1):
        arrived = auxg[i, pl.ds(HEADS, HEADS), :] * norm_g + auxg[i, pl.ds(0, HEADS), :]
        norm_g = jnp.where(i < g, arrived, norm_g)
    norm_in = decay_x * (decay_z * norm_g + norm_z) + norm_x
    for h in range(HEADS):
        lead = jnp.exp(-run_col[h])
        from_norm = jnp.sum(phiq[h].astype(F32) * norm_in[h : h + 1, :], axis=1, keepdims=True)
        inverse = 1.0 / (den[h] + lead * from_norm)
        o_ref[:, lanes(h)] = o_ref[:, lanes(h)] * inverse - t_ref[:, lanes(h)].astype(F32)
        den[h] = lead * inverse

    for c in inward[HALF:]:
        forward(c)

    def finish(p, states):
        for e in range(PER_X):
            h = PER_X * p + e
            state = states[pl.ds(e * PER_HEAD, PER_HEAD)].reshape(T, T)
            high = state.astype(BF16)
            low = (state - high.astype(F32)).astype(BF16)
            phi = phiq[h]
            at = pl.ds(pl.multiple_of(h * T, T), T)
            product = dot(jnp.concatenate([phi, phi], axis=1), jnp.concatenate([high, low], axis=0))
            o_ref[:, at] = o_ref[:, at] + den[h] * product

    finish(x, vout.at[x])
    for p in (other_x[1], other_x[2], other_x[0]):
        copy(vout.at[0], fin.at[p], s_v.at[0], r_v.at[p], at_x(p)).wait_recv()
        finish(p, fin.at[p])

    to = at_x(other_x[0])
    copy(own.at[three], xin.at[three], s_x.at[0], r_x.at[0], to).wait_send()
    copy(vout.at[three], fin.at[three], s_v.at[0], r_v.at[0], to).wait_send()
    copy(tout.at[seven], zin.at[seven], s_z.at[0], r_z.at[0], at_z(other_z[0])).wait_send()
    copy(wout.at[seven], cin.at[seven], s_w.at[0], r_w.at[0], at_z(other_z[0])).wait_send()
    to_later(lambda n: totals_of(n).wait_send())
    to_later(lambda n: sums_of(n).wait_send())
    copy(auxz.at[seven], auxz.at[seven], s_az.at[0], r_az.at[0], at_z(other_z[0])).wait_send()


def local(query_rows, key_rows, value_rows, teacher, query_map, key_map, decay_rate):
    rows = query_rows.shape[1:]
    operands = (
        query_rows.reshape(rows),
        key_rows.reshape(rows),
        value_rows.reshape(rows),
        teacher.reshape(rows),
        jnp.swapaxes(query_map, 1, 2),
        jnp.swapaxes(key_map, 1, 2),
        decay_rate.reshape(decay_rate.shape[1:]),
    )
    dma = lambda n: pltpu.SemaphoreType.DMA((n,))
    part = lambda *lead: pltpu.VMEM(lead + (SLICE, T), F32)
    rowed = lambda *lead: pltpu.VMEM(lead + (T,), F32)
    out = pl.pallas_call(
        kernel,
        out_shape=jax.ShapeDtypeStruct(rows, F32),
        in_specs=[pl.BlockSpec(memory_space=pltpu.HBM)] * 7,
        out_specs=pl.BlockSpec(memory_space=pltpu.VMEM),
        scratch_shapes=[pltpu.VMEM(a.shape, a.dtype) for a in operands]
        + [
            rowed(NX, QUARTER), rowed(NX, QUARTER),
            part(NZ), part(NZ), part(NG), rowed(NZ, AUX), rowed(NG, AUX),
            part(NZ), part(NZ), part(NX, NZ), part(NX, NZ),
            pltpu.VMEM((HEADS, T, T), BF16), pltpu.VMEM((HEADS, T, T), BF16),
            rowed(HEADS), rowed(HEADS, T), rowed(HEADS, T),
            dma(7), dma(1), dma(1), dma(1), dma(1), dma(1), dma(NZ + 1), dma(1), dma(1), dma(1), dma(1),
            dma(1), dma(NZ), dma(1), dma(NX),
        ],
        compiler_params=pltpu.CompilerParams(
            collective_id=0, has_side_effects=True, vmem_limit_bytes=32 * 1024 * 1024
        ),
    )(*[pltpu.with_memory_space_constraint(a, pltpu.HBM) for a in operands])
    return out.reshape(query_rows.shape)


def solution(mesh):
    rows = P(None, ("grp", "seq"), None)
    return jax.shard_map(
        local,
        mesh=mesh,
        in_specs=(rows, rows, rows, rows, P(), P(), P(None, None, ("grp", "seq"))),
        out_specs=rows,
        check_vma=False,
    )
```
